32 devices in a mesh: lsec: 8 (over z, x), rsec: 4 (over y, core).
Axes of the slice: x: 2, y: 2, z: 4, core: 2. Of those that a mesh axis runs over, the one named last changes fastest.
Arguments:
- wavefunction: bfloat16 [2, 8192, 8192], P(None, 'lsec', 'rsec'), may hold values from -6 to 6
- left_tiles: bfloat16 [4, 64, 2, 128, 128], P(None, 'lsec'), may hold values from -0.5 to 0.5
- left_source_sector: int32 [4, 64, 2], replicated, may hold values from 0 to 63
- left_weight: float32 [4, 64, 2], replicated, may hold values from -1 to 1
- left_sizes: int32 [64], replicated, may hold values from 1 to 128, 4096 in all
- right_tiles: bfloat16 [4, 64, 4, 128, 128], P(None, 'rsec'), may hold values from -0.5 to 0.5
- right_source: int32 [4, 64, 4], P(None, 'rsec'), may hold values from 0 to 63
- right_weight: float32 [4, 64, 4], P(None, 'rsec'), may hold values from -1 to 1
- right_sizes: int32 [64], replicated, may hold values from 1 to 128, 4096 in all
Outputs:
- sigma: bfloat16 [2, 8192, 8192], P(None, 'lsec', 'rsec')
The draws below stay inside these ranges and needn't reach their ends.
Inputs may be any that keep to these rules, and one draw needn't show every extreme that they name: `left_sizes`: left sector sizes sum to 4096; the largest is exactly 128. `right_sizes`: right sector sizes sum to 4096; the largest is exactly 128.
All inputs are finite; a program needn't handle non-finite values.
Results may differ from the reference program's by a relative error of at most 0.0064.
Values may be sent and summed in bfloat16 or wider, within the bound.
No kernel may reach another device: no remote copies, remote signals or barrier semaphores. Data moves between devices by JAX's collectives and lax.ppermute only.
A program may use at most 320 MiB of HBM per device.

```python
import math
import jax
import jax.numpy as jnp
import numpy as np
from jax import lax

S = 128
NL = 64
NR = 64
BOND = 4096
K = 4
NBL = 2
NBR = 4
DL = 8192
DR = 8192


def with_ends(drawn, rng, smallest, top_value):
    longest = drawn.shape.index(max(drawn.shape))
    spots = []
    for shift in (0, 1):
        where = [jax.random.randint(jax.random.fold_in(rng, axis), (), 0, length) for axis, length in enumerate(drawn.shape)]
        where[longest] = (where[longest] + shift) % drawn.shape[longest]
        spots.append(tuple(where))
    return drawn.at[spots[0]].set(smallest).at[spots[1]].set(top_value)


def level_of(own_key, extent, pieces, smallest, high):
    gain = 1.0
    for dim, parts in pieces:
        steps = jax.random.uniform(jax.random.fold_in(jax.random.fold_in(own_key, 6), dim), (parts,), jnp.float32, smallest / len(pieces), high / len(pieces))
        gain = gain * jnp.repeat(jnp.exp(steps), extent[dim] // parts).reshape((-1,) + (1,) * (len(extent) - 1 - dim))
    return gain


def profile(amount, total, bound, lean):
    loads = [(1 << 20) // math.isqrt(rank ** lean) + 1 for rank in range(2, amount + 1)]
    surplus, holding = total - bound - (amount - 1), [1] * (amount - 1)
    while surplus > 0:
        candidates = [i for i in range(amount - 1) if holding[i] < bound]
        pool, budget = sum([loads[i] for i in candidates]), surplus
        for i in candidates:
            extra = min(bound - holding[i], max(1, budget * loads[i] // pool), surplus)
            holding[i] = holding[i] + extra
            surplus = surplus - extra
    return np.array([bound] + holding)


def ragged_sizes(own_key, count, total, limit, lean):
    if count == 2:
        one = jax.random.randint(own_key, (), max(1, total - limit), min(limit, total - 1) + 1)
        return jnp.stack([one, total - one])
    sizes = jnp.asarray(profile(count, total, limit, lean), jnp.int32)
    pairs = (count - 1) // 2
    source_of, taker = sizes[1:1 + 2 * pairs:2], sizes[2:2 + 2 * pairs:2]
    margin = jnp.minimum(source_of - 1, limit - taker)
    shifted = jax.random.randint(jax.random.fold_in(own_key, 1), (pairs,), 0, 1 << 20) % (margin + 1)
    sizes = sizes.at[1:1 + 2 * pairs:2].set(source_of - shifted).at[2:2 + 2 * pairs:2].set(taker + shifted)
    return sizes[jax.random.permutation(jax.random.fold_in(own_key, 2), count)]


def centred(own_key, extent, width, reach, split=(), kind=jnp.bfloat16):
    values = width * jax.random.normal(own_key, extent, jnp.float32)
    if split:
        values = values * level_of(own_key, extent, split, -0.22, 0.18)
    return jnp.clip(values, -reach, reach).astype(kind)


def setup_inputs(seed: int = 0) -> dict:
    streams_of = jax.random.split(jax.random.key(seed), 10)
    wavefunction = centred(streams_of[0], (2, DL, DR), 1.0, 6.0, ((1, 8), (2, 4)))
    left_tiles = centred(streams_of[1], (K, NL, NBL, S, S), S ** -0.5, 0.5, ((1, 8),))
    left_source_sector = with_ends(jax.random.randint(streams_of[2], (K, NL, NBL), 0, NL), jax.random.fold_in(streams_of[2], 1), 0, NL - 1).astype(jnp.int32)
    left_weight = jnp.clip(jax.random.uniform(streams_of[3], (K, NL, NBL), jnp.float32, -1.0, 1.0), -1.0, 1.0)
    left_sizes = ragged_sizes(streams_of[4], NL, BOND, S, 2).astype(jnp.int32)
    right_tiles = centred(streams_of[5], (K, NR, NBR, S, S), S ** -0.5, 0.5, ((1, 4),))
    right_source = with_ends(jax.random.randint(streams_of[6], (K, NR, NBR), 0, NR), jax.random.fold_in(streams_of[6], 1), 0, NR - 1).astype(jnp.int32)
    right_weight = jnp.clip(jax.random.uniform(streams_of[7], (K, NR, NBR), jnp.float32, -1.0, 1.0) * level_of(streams_of[7], (K, NR, NBR), ((1, 4),), -0.4, 0.0), -1.0, 1.0)
    right_sizes = ragged_sizes(streams_of[8], NR, BOND, S, 2).astype(jnp.int32)
    return {"wavefunction": wavefunction, "left_tiles": left_tiles, "left_source_sector": left_source_sector, "left_weight": left_weight, "left_sizes": left_sizes, "right_tiles": right_tiles, "right_source": right_source, "right_weight": right_weight, "right_sizes": right_sizes}


def sector_mask(sizes, tile):
    offsets = jnp.arange(tile, dtype=jnp.int32)
    return (offsets[None, :] < sizes[:, None]).reshape(-1)


def scale_tile_stack(product_fragments, coupling_scale):
    scaled = (product_fragments.astype(jnp.float32) * coupling_scale[:, None, None]).astype(jnp.bfloat16)
    scaled = lax.optimization_barrier(scaled)
    return scaled.astype(jnp.float32)


def right_products(sector_block_list, source, weight, tiles):
    def one_sector(item):
        picks, coupling_scale, product_fragments = item
        selected_rows = jnp.take(sector_block_list, picks, axis=1).astype(jnp.float32)
        return jnp.einsum("fve,vue->fu", selected_rows, scale_tile_stack(product_fragments, coupling_scale))
    return lax.map(one_sector, (source, weight, tiles))


def left_products(rows, source, weight, tiles):
    def one_sector(item):
        picks, coupling_scale, product_fragments = item
        selected_rows = jnp.take(rows, picks, axis=0).astype(jnp.float32)
        return jnp.einsum("bij,bjc->ic", scale_tile_stack(product_fragments, coupling_scale), selected_rows)
    return lax.map(one_sector, (source, weight, tiles))


def reference(wavefunction, left_tiles, left_source_sector, left_weight, left_sizes, right_tiles, right_source, right_weight, right_sizes):
    keep = sector_mask(left_sizes, S)[:, None] & sector_mask(right_sizes, S)[None, :]
    results = []
    for vector in range(wavefunction.shape[0]):
        masked = jnp.where(keep, wavefunction[vector], jnp.zeros((), wavefunction.dtype))
        sector_block_list = masked.reshape(NL * S, NR, S)
        total = jnp.zeros((NL, S, NR * S), jnp.float32)
        for term in range(K):
            columns = right_products(sector_block_list, right_source[term], right_weight[term], right_tiles[term])
            product = jnp.transpose(columns, (1, 0, 2)).reshape(NL * S, NR * S).astype(jnp.bfloat16)
            total = total + left_products(product.reshape(NL, S, NR * S), left_source_sector[term], left_weight[term], left_tiles[term])
        total = jnp.where(keep, total.reshape(NL * S, NR * S), jnp.zeros((), total.dtype))
        results.append(total.astype(jnp.bfloat16))
    return jnp.stack(results)
```

```python
import functools

import jax
import jax.numpy as jnp
from jax import lax
from jax.experimental import pallas as pl
from jax.experimental.pallas import tpu as pltpu
from jax.sharding import PartitionSpec as P

F32 = jnp.float32
BF16 = jnp.bfloat16
I32 = jnp.int32
WIN = 256
VMEM_LIMIT = 60 * 1024 * 1024


def sector_mask(sizes, tile):
    offsets = jnp.arange(tile, dtype=jnp.int32)
    return (offsets[None, :] < sizes[:, None]).reshape(-1)


def scaled_tiles(tiles, weight):
    return (tiles.astype(jnp.float32) * weight[..., None, None]).astype(jnp.bfloat16)


def weighted_right(selected_rows, scaled):
    return jnp.einsum("vlqbs,qbts->vlqt", selected_rows, scaled, preferred_element_type=jnp.float32)


def left_rows(arranged, product_fragments, source, weight):
    total = None
    for term in range(product_fragments.shape[0]):
        selected_rows = jnp.take(arranged[:, :, :, term, :], source[term], axis=1)
        scaled = scaled_tiles(product_fragments[term], weight[term])
        part = jnp.einsum(
            "mbij,vmbjc->vmic", scaled, selected_rows, preferred_element_type=jnp.float32
        )
        total = part if total is None else total + part
    return total.reshape(total.shape[0], -1, total.shape[-1])


def general(
    wavefunction,
    left_tiles,
    left_source_sector,
    left_weight,
    left_sizes,
    right_tiles,
    right_source,
    right_weight,
    right_sizes,
):
    vectors, rows_local, cols_local = wavefunction.shape
    terms_count = right_tiles.shape[0]
    tile = right_tiles.shape[3]
    left_count = left_sizes.shape[0]
    right_count = right_sizes.shape[0]
    left_local = rows_local // tile
    right_local = cols_local // tile
    left_devices = lax.axis_size("lsec")
    width = cols_local // left_devices
    left_place = lax.axis_index("lsec")
    right_place = lax.axis_index("rsec")
    row_keep_mask = sector_mask(
        lax.dynamic_slice_in_dim(left_sizes, left_place * left_local, left_local), tile
    )
    col_keep = sector_mask(
        lax.dynamic_slice_in_dim(right_sizes, right_place * right_local, right_local), tile
    )
    masked = jnp.where(
        row_keep_mask[None, :, None] & col_keep[None, None, :],
        wavefunction,
        jnp.zeros((), wavefunction.dtype),
    )
    right_scaled = scaled_tiles(right_tiles, right_weight)
    gathered = lax.all_gather(masked, "rsec", axis=2, tiled=True)
    sector_block_list = gathered.reshape(vectors, rows_local, right_count, tile)
    products = []
    for term in range(terms_count):
        selected_rows = jnp.take(sector_block_list, right_source[term], axis=2)
        products.append(weighted_right(selected_rows, right_scaled[term]))
    rounded = [
        item.astype(jnp.bfloat16).reshape(vectors, rows_local, left_devices, width)
        for item in products
    ]
    outgoing = jnp.stack(rounded, axis=3)
    exchanged_values = lax.all_to_all(
        outgoing.reshape(vectors, rows_local, -1), "lsec", split_axis=2, concat_axis=1, tiled=True
    )
    arranged = exchanged_values.reshape(vectors, left_count, tile, terms_count, width)
    sigma_part = left_rows(
        arranged,
        lax.all_gather(left_tiles, "lsec", axis=1, tiled=True),
        left_source_sector,
        left_weight,
    )
    row_all = sector_mask(left_sizes, tile)
    columns = right_place * cols_local + left_place * width + jnp.arange(width, dtype=jnp.int32)
    column_sizes = jnp.take(right_sizes, columns // tile)
    column_keep = columns % tile < column_sizes
    result = jnp.where(
        row_all[None, :, None] & column_keep[None, None, :],
        sigma_part,
        jnp.zeros((), sigma_part.dtype),
    )
    return lax.all_to_all(
        result.astype(jnp.bfloat16), "lsec", split_axis=1, concat_axis=2, tiled=True
    )


def exclusive(values):
    return jnp.cumsum(values, axis=-1) - values


def one_hot(index, count):
    return (index[..., None] == jnp.arange(count, dtype=I32)).astype(BF16)


def lookup(table, index):
    return jnp.sum(jnp.where(index[..., None] == jnp.arange(table.shape[0], dtype=I32), table, 0), axis=-1)


def matmul(a, b):
    return jnp.matmul(a, b, preferred_element_type=F32)


def cost(flops, bytes_accessed):
    return pl.CostEstimate(flops=int(flops), bytes_accessed=int(bytes_accessed), transcendentals=0)


def build_kernel(dims, item_kb, item_lo, item_hi, item_win, item_shift, item_size, panel_first, panel_last, right_ref, *outs):
    widths, right_b, panels = dims
    tile = right_ref.shape[2]
    here = pl.program_id(0) * panels + pl.program_id(1)
    for out in outs:
        out[...] = jnp.zeros_like(out)
    lane = lax.broadcasted_iota(I32, (tile, WIN), 1) + pl.program_id(1) * WIN
    source = lax.broadcasted_iota(I32, (WIN, tile), 1)
    target = lax.broadcasted_iota(I32, (WIN, tile), 0) - source

    def step(it, carry):
        kb = item_kb[it]
        term = kb // right_b
        block = right_ref[0, kb].astype(F32)
        block = jnp.where((lane >= item_lo[it]) & (lane < item_hi[it]), block, 0.0).astype(BF16)
        shift = jnp.where((target == item_shift[it]) & (source < item_size[it]), 1.0, 0.0).astype(BF16)
        value = jnp.dot(shift, block, preferred_element_type=F32)
        for part in range(WIN // tile):
            start = item_win[it] + part * tile
            base = 0
            for out, width in zip(outs, widths):
                @pl.when((start >= base) & (start < base + width))
                def _(out=out, width=width, base=base):
                    row = pl.multiple_of(term * width + start - base, tile)
                    row = jnp.clip(row, 0, out.shape[1] - tile)
                    row = pl.multiple_of(row, tile)
                    out[0, pl.ds(row, tile), :] = (
                        out[0, pl.ds(row, tile), :].astype(F32) + value[part * tile : (part + 1) * tile]
                    ).astype(BF16)
                base += width
        return carry

    lax.fori_loop(panel_first[here], panel_last[here], step, 0)


def left_kernel(dims, place_ref, left_slot, left_start, row_start, *refs):
    chain, terms, steps, width = dims
    blocks = refs[: 2 * chain - 1]
    left_ref, out_ref, gathered, left_tiles, sem = refs[2 * chain - 1 :]
    tile = left_ref.shape[1]
    place = place_ref[0]

    def each(action):
        action(pltpu.make_async_copy(blocks[0], gathered.at[place], sem.at[0]))
        for d in range(1, chain):
            @pl.when(place - d >= 0)
            def _():
                action(pltpu.make_async_copy(blocks[d], gathered.at[jnp.maximum(place - d, 0)], sem.at[d]))

            @pl.when(place + d < chain)
            def _():
                action(
                    pltpu.make_async_copy(
                        blocks[chain - 1 + d], gathered.at[jnp.minimum(place + d, chain - 1)], sem.at[chain - 1 + d]
                    )
                )
        action(pltpu.make_async_copy(left_ref, left_tiles, sem.at[2 * chain - 1]))

    each(lambda copy: copy.start())
    out_ref[...] = jnp.zeros_like(out_ref)
    each(lambda copy: copy.wait())

    def sector_step(sector, carry):
        row = pl.multiple_of(row_start[sector], 16)
        for term in range(terms):
            i = sector * terms + term
            first_start = pl.multiple_of(left_start[2 * i], 16)
            second_start = pl.multiple_of(left_start[2 * i + 1], 16)
            for n in range(0, width, WIN):
                lanes = slice(n, min(n + WIN, width))
                value = jnp.dot(
                    left_tiles[i, :, :WIN],
                    gathered[left_slot[2 * i], pl.ds(first_start, WIN), lanes],
                    preferred_element_type=F32,
                ) + jnp.dot(
                    left_tiles[i, :, WIN:],
                    gathered[left_slot[2 * i + 1], pl.ds(second_start, WIN), lanes],
                    preferred_element_type=F32,
                )
                out_ref[pl.ds(row, tile), term * width + n : term * width + lanes.stop] = value.astype(BF16)
        return carry

    lax.fori_loop(0, steps, sector_step, 0)


def right_kernel(dims, half_ref, rows_ref, slot_cols, left_ref, right_ref, *refs):
    chunk, added = dims
    out_ref = refs[-1]
    columns = slot_cols[pl.program_id(0)] - pl.program_id(1) * WIN
    count = jnp.where(columns > 0, (rows_ref[0] + chunk - 1) // chunk, 0)

    def compute(m, carry):
        row = pl.multiple_of(m * chunk, chunk)
        value = jnp.dot(left_ref[pl.ds(row, chunk), :], right_ref[0], preferred_element_type=F32)
        if added:
            value = value + refs[0][0, pl.ds(row, chunk), :].astype(F32)
        out_ref[0, pl.ds(row, chunk), :] = value.astype(BF16)
        return carry

    def clear(m, carry):
        row = pl.multiple_of(m * chunk, chunk)
        out_ref[0, pl.ds(row, chunk), :] = jnp.zeros((chunk, out_ref.shape[2]), BF16)
        return carry

    lax.fori_loop(0, count, compute, 0)
    lax.fori_loop(count, out_ref.shape[1] // chunk, clear, 0)


def fast(caps, wavefunction, left_tiles, left_source, left_weight, left_sizes, right_tiles, right_source, right_weight, right_sizes):
    cap_row, cap_pair, cap_half, cap_col = caps
    vectors, rows_local, cols_local = wavefunction.shape
    terms, right_local, right_b, tile, _ = right_tiles.shape
    left_b = left_tiles.shape[2]
    left_devices = lax.axis_size("lsec")
    right_devices = lax.axis_size("rsec")
    left_local = rows_local // tile
    chain = left_devices // 2
    height = right_devices // 2
    left_place = lax.axis_index("lsec")
    right_place = lax.axis_index("rsec")
    side = left_place % 2
    place = left_place // 2
    core = right_place % 2
    tall = right_place // 2
    swap_side = [(i, i ^ 1) for i in range(left_devices)]
    swap_core = [(i, i ^ 1) for i in range(right_devices)]
    first_width = (cap_col // 128 + 1) // 2 * 128
    widths = [first_width, cap_col - first_width]
    bounds = [0, first_width, cap_col]

    own_sizes = lax.dynamic_slice_in_dim(left_sizes, left_place * left_local, left_local)
    pair_sizes = left_sizes.reshape(chain, 2 * left_local)
    pair_offset = exclusive(pair_sizes).reshape(-1)
    own_count = jnp.sum(own_sizes)
    rounded = (left_sizes + 15) // 16 * 16
    half_offset = exclusive(rounded.reshape(left_devices, left_local))
    half_count = jnp.sum(rounded.reshape(left_devices, left_local), axis=-1)
    column_offset = exclusive(right_sizes.reshape(right_devices, right_local)).reshape(-1)
    column_count = jnp.sum(right_sizes.reshape(right_devices, right_local), axis=-1)
    offsets = jnp.arange(tile, dtype=I32)

    def spread(starts, sizes):
        return jnp.where(offsets[None, :] < sizes[:, None], starts[:, None] + offsets[None, :], -1).reshape(-1)

    own_right = right_place * right_local
    col_sizes = lax.dynamic_slice_in_dim(right_sizes, own_right, right_local)
    col_starts = lax.dynamic_slice_in_dim(column_offset, own_right, right_local)
    col_select = one_hot(spread(col_starts, col_sizes), cap_col)
    pair_starts = lax.dynamic_slice_in_dim(pair_offset, left_place * left_local, left_local)
    local_index = spread(exclusive(own_sizes), own_sizes)
    pair_index = spread(pair_starts, own_sizes)

    with jax.named_scope("pack"):
        mine = lax.dynamic_index_in_dim(wavefunction, side, 0, keepdims=False)
        other = lax.dynamic_index_in_dim(wavefunction, 1 - side, 0, keepdims=False)
        other_rows = matmul(one_hot(local_index, cap_row).T, other).astype(BF16)
        mine_rows = matmul(one_hot(pair_index, cap_pair).T, mine).astype(BF16)
        pair_total = jnp.sum(lax.dynamic_index_in_dim(pair_sizes, place, 0, keepdims=False))
        partner_base = jnp.where(side == 0, own_count, 0)
        partner_count = pair_total - own_count
        spots = jnp.arange(cap_row, dtype=I32)
        partner_select = one_hot(jnp.where(spots < partner_count, partner_base + spots, -1), cap_pair).T
        incoming = []
        for n in range(2):
            outgoing = matmul(other_rows, col_select[:, bounds[n] : bounds[n + 1]]).astype(BF16)
            incoming.append(lax.ppermute(outgoing, "lsec", swap_side))
        pair = []
        for n in range(2):
            own_part = matmul(mine_rows, col_select[:, bounds[n] : bounds[n + 1]])
            pair.append((own_part + matmul(partner_select, incoming[n])).astype(BF16))

    with jax.named_scope("right_exchange"):
        scaled = (right_tiles.astype(F32) * right_weight[..., None, None]).astype(BF16)
        compact = jnp.einsum(
            "kqbts,qtc->kbsc", scaled, col_select.reshape(right_local, tile, cap_col), preferred_element_type=F32
        ).astype(BF16).reshape(terms * right_b, tile, cap_col)
        near = jnp.stack([compact, lax.ppermute(compact, "rsec", swap_core)])
        pieces = []
        for d in range(1, height):
            piece = lax.ppermute(
                compact, "rsec", [(i, ((i // 2 - d) % height) * 2 + i % 2) for i in range(right_devices)]
            )
            pieces = pieces + [piece, lax.ppermute(piece, "rsec", swap_core)]
        far = jnp.stack(pieces) if pieces else None

    with jax.named_scope("left_exchange"):
        own_weight = lax.dynamic_slice_in_dim(left_weight, left_place * left_local, left_local, 1)
        left_scaled = (left_tiles.astype(F32) * own_weight[..., None, None]).astype(BF16)
        left_other = lax.ppermute(left_scaled, "lsec", swap_side)
        left_pair = jnp.where(
            side == 0, jnp.concatenate([left_scaled, left_other], 1), jnp.concatenate([left_other, left_scaled], 1)
        )
        source = lax.dynamic_slice_in_dim(left_source, place * 2 * left_local, 2 * left_local, 1)
        source = jnp.transpose(source, (1, 0, 2))
        source_offset = lookup(pair_offset, source)
        left_slot = source // (2 * left_local)
        left_start = jnp.minimum(source_offset // 16 * 16, cap_pair - WIN)
        source_size = lookup(left_sizes, source)
        moved = jnp.where(
            offsets < source_size[..., None], (source_offset - left_start)[..., None] + offsets, -1
        )
        left_shifted = jnp.einsum(
            "klbij,lkbjc->lkibc", left_pair, one_hot(moved, WIN), preferred_element_type=F32
        ).astype(BF16).reshape(2 * left_local * terms, tile, left_b * WIN)

    with jax.named_scope("chain"):
        upward = [[part] for part in pair]
        downward = [[part] for part in pair]
        for _ in range(1, chain):
            for n in range(2):
                upward[n].append(
                    lax.ppermute(upward[n][-1], "lsec", [(i, i + 2) for i in range(left_devices - 2)])
                )
                downward[n].append(
                    lax.ppermute(downward[n][-1], "lsec", [(i + 2, i) for i in range(left_devices - 2)])
                )

    with jax.named_scope("lists"):
        source_all = lax.all_gather(right_source, "rsec", axis=1, tiled=True)
        source_all = jnp.transpose(source_all.reshape(terms, right_devices, right_local, right_b), (1, 2, 0, 3))
        slots = jnp.arange(right_devices, dtype=I32)
        groups = 2 * ((tall + slots // 2) % height) + (core + slots) % 2
        ordered = jnp.stack(
            [lax.dynamic_index_in_dim(source_all, groups[s], 0, keepdims=False) for s in range(right_devices)]
        ).reshape(-1)
        items = ordered.shape[0]
        per_sector = terms * right_b
        per_slot = right_local * per_sector
        number = jnp.arange(items, dtype=I32)
        key = jnp.where(ordered // right_local == right_place, number, items + number)
        key, ordered = lax.sort((key, ordered), num_keys=1)
        active = key < items
        number = key % items
        item_slot = number // per_slot
        sector = (2 * ((tall + item_slot // 2) % height) + (core + item_slot) % 2) * right_local
        sector = sector + number // per_sector % right_local
        low = lookup(column_offset, sector)
        high = low + lookup(right_sizes, sector)
        from_offset = lookup(column_offset, ordered)
        window = jnp.minimum(from_offset // 128 * 128, cap_col - WIN)
        panels = (cap_col + WIN - 1) // WIN
        edges = jnp.arange(panels, dtype=I32) * WIN
        earlier = item_slot[None, None, :] < slots[:, None, None]
        same = item_slot[None, None, :] == slots[:, None, None]
        before = active & (earlier | (same & (high <= edges[None, :, None])))
        within = active & (earlier | (same & (low < edges[None, :, None] + WIN)))
        panel_first = jnp.sum(before.astype(I32), -1)
        panel_last = jnp.sum(within.astype(I32), -1)
        fields = (number % per_sector, low, high, window, from_offset - window, lookup(right_sizes, ordered))
        halves = lax.dynamic_slice_in_dim(half_offset, place * 2, 2, 0) + jnp.arange(2, dtype=I32)[:, None] * cap_half
        half_rows = lax.dynamic_slice_in_dim(half_count, place * 2, 2, 0)
        slot_cols = lookup(column_count, groups)

    anywhere = pl.BlockSpec(memory_space=pl.ANY)

    def build(right_some, from_slot):
        number_of = right_some.shape[0]
        scalars = (
            *fields,
            panel_first[from_slot : from_slot + number_of].reshape(-1),
            panel_last[from_slot : from_slot + number_of].reshape(-1),
        )
        return pl.pallas_call(
            functools.partial(build_kernel, (widths, right_b, panels)),
            out_shape=[jax.ShapeDtypeStruct((number_of, terms * width, cap_col), BF16) for width in widths],
            grid_spec=pltpu.PrefetchScalarGridSpec(
                num_scalar_prefetch=len(scalars),
                grid=(number_of, panels),
                in_specs=[pl.BlockSpec((1, per_sector, tile, WIN), lambda s, p, *_: (s, 0, 0, p))],
                out_specs=[pl.BlockSpec((1, terms * width, WIN), lambda s, p, *_: (s, 0, p)) for width in widths],
            ),
            compiler_params=pltpu.CompilerParams(vmem_limit_bytes=VMEM_LIMIT),
            cost_estimate=cost(4e9 * number_of, 20e6 * number_of),
        )(*scalars, right_some)

    with jax.named_scope("build"):
        built = [build(near, 0)]
        if far is not None:
            built.append(build(far, 2))

    rows = 2 * cap_half

    def apply_left(n):
        blocks = upward[n] + downward[n][1:]
        scalars = (place.reshape(1), left_slot.reshape(-1), left_start.reshape(-1), halves.reshape(-1))
        width = widths[n]
        return pl.pallas_call(
            functools.partial(left_kernel, (chain, terms, 2 * left_local, width)),
            out_shape=jax.ShapeDtypeStruct((rows + tile, terms * width), BF16),
            grid_spec=pltpu.PrefetchScalarGridSpec(
                num_scalar_prefetch=len(scalars),
                grid=(1,),
                in_specs=[anywhere] * (len(blocks) + 1),
                out_specs=pl.BlockSpec((rows + tile, terms * width), lambda i, *_: (0, 0)),
                scratch_shapes=[
                    pltpu.VMEM((chain, cap_pair, width), BF16),
                    pltpu.VMEM((2 * left_local * terms, tile, left_b * WIN), BF16),
                    pltpu.SemaphoreType.DMA((2 * chain,)),
                ],
            ),
            compiler_params=pltpu.CompilerParams(vmem_limit_bytes=VMEM_LIMIT),
            cost_estimate=cost(15e9, 30e6),
        )(*scalars, *blocks, left_shifted)

    def apply_right(n, half, product, part, added):
        number_of = part.shape[0]
        chunk = 256 if cap_half % 256 == 0 else 128
        width = terms * widths[n]
        first_slot = added[1]
        scalars = (
            half.reshape(1),
            lax.dynamic_index_in_dim(half_rows, half, 0),
            slot_cols[first_slot : first_slot + number_of],
        )
        block = pl.BlockSpec((1, cap_half, WIN), lambda s, p, *_: (s, 0, p))
        extra = [] if added[0] is None else [added[0]]
        return pl.pallas_call(
            functools.partial(right_kernel, (chunk, bool(extra))),
            out_shape=jax.ShapeDtypeStruct((number_of, cap_half, cap_col), BF16),
            grid_spec=pltpu.PrefetchScalarGridSpec(
                num_scalar_prefetch=len(scalars),
                grid=(number_of, panels),
                in_specs=[
                    pl.BlockSpec((cap_half, width), lambda s, p, half, *_: (half[0], 0)),
                    pl.BlockSpec((1, width, WIN), lambda s, p, *_: (s, 0, p)),
                ]
                + [block] * len(extra),
                out_specs=block,
            ),
            compiler_params=pltpu.CompilerParams(vmem_limit_bytes=VMEM_LIMIT),
            cost_estimate=cost(2 * 0.75 * cap_half * width * cap_col * number_of, number_of * width * cap_col * 2),
        )(*scalars, product, part, *extra)

    def reduce_half(partials):
        near_sum = partials[0][0].astype(F32) + lax.ppermute(partials[0][1], "rsec", swap_core).astype(F32)
        result = near_sum
        if far is not None:
            from_core = lax.ppermute(partials[1][1::2], "rsec", swap_core)
            for d in range(1, height):
                summed = partials[1][2 * d - 2].astype(F32) + from_core[d - 1].astype(F32)
                result = result + lax.ppermute(
                    summed.astype(BF16),
                    "rsec",
                    [(i, ((i // 2 + d) % height) * 2 + i % 2) for i in range(right_devices)],
                ).astype(F32)
        return result.astype(BF16)

    order = [1 - side, side]
    partials = [[(None, 2 * s) for s in range(len(built))] for _ in order]
    with jax.named_scope("apply"):
        for n in range(2):
            product = apply_left(n)
            for h in range(2):
                for s in range(len(built) - 1, -1, -1):
                    partials[h][s] = (
                        apply_right(n, order[h], product, built[s][n], partials[h][s]),
                        2 * s,
                    )
    with jax.named_scope("reduce"):
        given = reduce_half([item[0] for item in partials[0]])
        taken = lax.ppermute(given, "lsec", swap_side)
        kept = reduce_half([item[0] for item in partials[1]])

    with jax.named_scope("unpack"):
        own_half = lax.dynamic_index_in_dim(half_offset, left_place, 0, keepdims=False)
        row_select = one_hot(spread(own_half, own_sizes), cap_half)

        def expand(value):
            return matmul(matmul(row_select, value).astype(BF16), col_select.T).astype(BF16)

        kept = expand(kept)
        taken = expand(taken)
        return jnp.stack([jnp.where(side == 0, kept, taken), jnp.where(side == 0, taken, kept)])


def local(wavefunction, left_tiles, left_source, left_weight, left_sizes, right_tiles, right_source, right_weight, right_sizes):
    _, rows_local, cols_local = wavefunction.shape
    left_devices = lax.axis_size("lsec")
    right_devices = lax.axis_size("rsec")
    by_device = left_sizes.reshape(left_devices, -1)
    most_rows = jnp.max(jnp.sum(by_device, -1))
    most_half = jnp.max(jnp.sum((by_device + 15) // 16 * 16, -1))
    most_pair = jnp.max(jnp.sum(left_sizes.reshape(left_devices // 2, -1), -1))
    most_cols = jnp.max(jnp.sum(right_sizes.reshape(right_devices, -1), -1))
    arguments = (wavefunction, left_tiles, left_source, left_weight, left_sizes, right_tiles, right_source, right_weight, right_sizes)
    branches = [general]
    choice = jnp.zeros((), I32)
    for level, (row, pair, half, col) in enumerate(LEVELS):
        caps = (
            rows_local * row // 16,
            rows_local * pair // 16,
            rows_local * half // 16,
            cols_local * col // 16 // 128 * 128,
        )
        fits = (most_rows <= caps[0]) & (most_pair <= caps[1]) & (most_half <= caps[2]) & (most_cols <= caps[3])
        branches.append(functools.partial(fast, caps))
        choice = jnp.where(fits, level + 1, choice)
    return lax.switch(choice, branches, *arguments)


LEVELS = ((16, 24, 16, 12), (12, 20, 12, 10))


def solution(mesh):
    return jax.shard_map(
        local,
        mesh=mesh,
        in_specs=(
            P(None, "lsec", "rsec"),
            P(None, "lsec", None, None, None),
            P(),
            P(),
            P(),
            P(None, "rsec", None, None, None),
            P(None, "rsec", None),
            P(None, "rsec", None),
            P(),
        ),
        out_specs=P(None, "lsec", "rsec"),
        check_vma=False,
    )
```

```python
import functools

import jax
import jax.numpy as jnp
from jax import lax
from jax.experimental import pallas as pl
from jax.experimental.pallas import tpu as pltpu
from jax.sharding import PartitionSpec as P

F32 = jnp.float32
BF16 = jnp.bfloat16
I32 = jnp.int32
WIN = 256
VMEM_LIMIT = 60 * 1024 * 1024


def sector_mask(sizes, tile):
    offsets = jnp.arange(tile, dtype=jnp.int32)
    return (offsets[None, :] < sizes[:, None]).reshape(-1)


def scaled_tiles(tiles, weight):
    return (tiles.astype(jnp.float32) * weight[..., None, None]).astype(jnp.bfloat16)


def weighted_right(selected_rows, scaled):
    return jnp.einsum("vlqbs,qbts->vlqt", selected_rows, scaled, preferred_element_type=jnp.float32)


def left_rows(arranged, product_fragments, source, weight):
    total = None
    for term in range(product_fragments.shape[0]):
        selected_rows = jnp.take(arranged[:, :, :, term, :], source[term], axis=1)
        scaled = scaled_tiles(product_fragments[term], weight[term])
        part = jnp.einsum(
            "mbij,vmbjc->vmic", scaled, selected_rows, preferred_element_type=jnp.float32
        )
        total = part if total is None else total + part
    return total.reshape(total.shape[0], -1, total.shape[-1])


def general(
    wavefunction,
    left_tiles,
    left_source_sector,
    left_weight,
    left_sizes,
    right_tiles,
    right_source,
    right_weight,
    right_sizes,
):
    vectors, rows_local, cols_local = wavefunction.shape
    terms_count = right_tiles.shape[0]
    tile = right_tiles.shape[3]
    left_count = left_sizes.shape[0]
    right_count = right_sizes.shape[0]
    left_local = rows_local // tile
    right_local = cols_local // tile
    left_devices = lax.axis_size("lsec")
    width = cols_local // left_devices
    left_place = lax.axis_index("lsec")
    right_place = lax.axis_index("rsec")
    row_keep_mask = sector_mask(
        lax.dynamic_slice_in_dim(left_sizes, left_place * left_local, left_local), tile
    )
    col_keep = sector_mask(
        lax.dynamic_slice_in_dim(right_sizes, right_place * right_local, right_local), tile
    )
    masked = jnp.where(
        row_keep_mask[None, :, None] & col_keep[None, None, :],
        wavefunction,
        jnp.zeros((), wavefunction.dtype),
    )
    right_scaled = scaled_tiles(right_tiles, right_weight)
    gathered = lax.all_gather(masked, "rsec", axis=2, tiled=True)
    sector_block_list = gathered.reshape(vectors, rows_local, right_count, tile)
    products = []
    for term in range(terms_count):
        selected_rows = jnp.take(sector_block_list, right_source[term], axis=2)
        products.append(weighted_right(selected_rows, right_scaled[term]))
    rounded = [
        item.astype(jnp.bfloat16).reshape(vectors, rows_local, left_devices, width)
        for item in products
    ]
    outgoing = jnp.stack(rounded, axis=3)
    exchanged_values = lax.all_to_all(
        outgoing.reshape(vectors, rows_local, -1), "lsec", split_axis=2, concat_axis=1, tiled=True
    )
    arranged = exchanged_values.reshape(vectors, left_count, tile, terms_count, width)
    sigma_part = left_rows(
        arranged,
        lax.all_gather(left_tiles, "lsec", axis=1, tiled=True),
        left_source_sector,
        left_weight,
    )
    row_all = sector_mask(left_sizes, tile)
    columns = right_place * cols_local + left_place * width + jnp.arange(width, dtype=jnp.int32)
    column_sizes = jnp.take(right_sizes, columns // tile)
    column_keep = columns % tile < column_sizes
    result = jnp.where(
        row_all[None, :, None] & column_keep[None, None, :],
        sigma_part,
        jnp.zeros((), sigma_part.dtype),
    )
    return lax.all_to_all(
        result.astype(jnp.bfloat16), "lsec", split_axis=1, concat_axis=2, tiled=True
    )


def exclusive(values):
    return jnp.cumsum(values, axis=-1) - values


def one_hot(index, count):
    return (index[..., None] == jnp.arange(count, dtype=I32)).astype(BF16)


def lookup(table, index):
    return jnp.sum(jnp.where(index[..., None] == jnp.arange(table.shape[0], dtype=I32), table, 0), axis=-1)


def matmul(a, b):
    return jnp.matmul(a, b, preferred_element_type=F32)


def after(value, *others):
    return lax.optimization_barrier((value, others))[0]


def cost(flops, bytes_accessed):
    return pl.CostEstimate(flops=int(flops), bytes_accessed=int(bytes_accessed), transcendentals=0)


def compact_kernel(start_ref, tiles_ref, out_ref, rows_ref):
    tile = tiles_ref.shape[3]

    @pl.when((pl.program_id(0) == 0) & (pl.program_id(1) == 0))
    def _():
        rows_ref[...] = jnp.zeros_like(rows_ref)

    for q in range(tiles_ref.shape[1]):
        rows_ref[pl.ds(start_ref[q], tile), :] = tiles_ref[0, q, 0].astype(F32)
    out_ref[0] = rows_ref[: out_ref.shape[1], :].astype(BF16)


def build_kernel(dims, item_kb, item_lo, item_hi, item_win, item_shift, item_size, item_weight, panel_first, panel_last, *refs):
    widths, right_b, panels, split, items = dims
    outs = refs[-1 - len(widths) : -1]
    held = refs[-1]
    parts = refs[: -1 - len(widths)]
    tile = held.shape[2]
    here = pl.program_id(0) * panels + pl.program_id(1)
    for slot in range(2):
        @pl.when(pl.program_id(0) == slot)
        def _(slot=slot):
            base = 0
            for part in parts[slot * split : (slot + 1) * split]:
                held[base : base + part.shape[0]] = part[...]
                base += part.shape[0]

    for out in outs:
        out[...] = jnp.zeros_like(out)
    column = lax.broadcasted_iota(I32, (WIN, tile), 0) + pl.program_id(1) * WIN
    source = lax.broadcasted_iota(I32, (WIN, tile), 1)
    target = lax.broadcasted_iota(I32, (WIN, tile), 0) - source
    first = panel_first[here]
    last = panel_last[here]

    def step(g, carry):
        values = []
        for u in range(2):
            raw = first + 2 * g + u
            it = jnp.minimum(raw, items - 1)
            kb = item_kb[it]
            block = (held[kb].astype(F32) * item_weight[it])
            block = jnp.where((column >= item_lo[it]) & (column < item_hi[it]), block, 0.0).astype(BF16)
            size = jnp.where(raw < last, item_size[it], 0)
            shift = jnp.where((target == item_shift[it]) & (source < size), 1.0, 0.0).astype(BF16)
            value = lax.dot_general(shift, block, (((1,), (1,)), ((), ())), preferred_element_type=F32)
            values.append((kb // right_b, item_win[it], value.astype(BF16)))
        for term, window, value in values:
            for part in range(WIN // tile):
                start = window + part * tile
                base = 0
                for out, width in zip(outs, widths):
                    @pl.when((start >= base) & (start < base + width))
                    def _(out=out, width=width, base=base, part=part, term=term, start=start, value=value):
                        row = jnp.clip(term * width + start - base, 0, out.shape[0] - tile)
                        row = pl.multiple_of(row, tile)
                        out[pl.ds(row, tile), :] += value[part * tile : (part + 1) * tile]
                    base += width
        return carry

    lax.fori_loop(0, (last - first + 1) // 2, step, 0)


def left_kernel(dims, place_ref, left_slot, left_start, row_start, *refs):
    chain, terms, steps, width = dims
    blocks = refs[: 2 * chain - 1]
    left_ref, out_ref, gathered, left_tiles, sem = refs[2 * chain - 1 :]
    tile = left_ref.shape[2]
    place = place_ref[0]

    def each(action):
        action(pltpu.make_async_copy(blocks[0], gathered.at[place], sem.at[0]))
        for d in range(1, chain):
            @pl.when(place - d >= 0)
            def _():
                action(pltpu.make_async_copy(blocks[d], gathered.at[jnp.maximum(place - d, 0)], sem.at[d]))

            @pl.when(place + d < chain)
            def _():
                action(
                    pltpu.make_async_copy(
                        blocks[chain - 1 + d], gathered.at[jnp.minimum(place + d, chain - 1)], sem.at[chain - 1 + d]
                    )
                )
        action(pltpu.make_async_copy(left_ref, left_tiles, sem.at[2 * chain - 1]))

    each(lambda copy: copy.start())
    out_ref[...] = jnp.zeros_like(out_ref)
    each(lambda copy: copy.wait())

    def sector_step(sector, carry):
        row = pl.multiple_of(row_start[sector], 16)
        for term in range(terms):
            i = sector * terms + term
            first_start = pl.multiple_of(left_start[2 * i], 16)
            second_start = pl.multiple_of(left_start[2 * i + 1], 16)
            for n in range(0, width, WIN):
                lanes = slice(n, min(n + WIN, width))
                value = jnp.dot(
                    left_tiles[i, 0],
                    gathered[left_slot[2 * i], pl.ds(first_start, WIN), lanes],
                    preferred_element_type=F32,
                ) + jnp.dot(
                    left_tiles[i, 1],
                    gathered[left_slot[2 * i + 1], pl.ds(second_start, WIN), lanes],
                    preferred_element_type=F32,
                )
                out_ref[pl.ds(row, tile), term * width + n : term * width + lanes.stop] = value.astype(BF16)
        return carry

    lax.fori_loop(0, steps, sector_step, 0)


def fast(caps, wavefunction, left_tiles, left_source, left_weight, left_sizes, right_tiles, right_source, right_weight, right_sizes):
    cap_row, cap_pair, cap_half, cap_col = caps
    vectors, rows_local, cols_local = wavefunction.shape
    terms, right_local, right_b, tile, _ = right_tiles.shape
    left_b = left_tiles.shape[2]
    left_devices = lax.axis_size("lsec")
    right_devices = lax.axis_size("rsec")
    left_local = rows_local // tile
    chain = left_devices // 2
    height = right_devices // 2
    left_place = lax.axis_index("lsec")
    right_place = lax.axis_index("rsec")
    side = left_place % 2
    place = left_place // 2
    core = right_place % 2
    tall = right_place // 2
    swap_side = [(i, i ^ 1) for i in range(left_devices)]
    swap_core = [(i, i ^ 1) for i in range(right_devices)]
    first_width = (cap_col // 128 + 1) // 2 * 128
    widths = [first_width, cap_col - first_width]
    bounds = [0, first_width, cap_col]

    own_sizes = lax.dynamic_slice_in_dim(left_sizes, left_place * left_local, left_local)
    pair_sizes = left_sizes.reshape(chain, 2 * left_local)
    pair_offset = exclusive(pair_sizes).reshape(-1)
    own_count = jnp.sum(own_sizes)
    rounded = (left_sizes + 15) // 16 * 16
    half_offset = exclusive(rounded.reshape(left_devices, left_local))
    half_count = jnp.sum(rounded.reshape(left_devices, left_local), axis=-1)
    column_offset = exclusive(right_sizes.reshape(right_devices, right_local)).reshape(-1)
    column_count = jnp.sum(right_sizes.reshape(right_devices, right_local), axis=-1)
    offsets = jnp.arange(tile, dtype=I32)

    def spread(starts, sizes):
        return jnp.where(offsets[None, :] < sizes[:, None], starts[:, None] + offsets[None, :], -1).reshape(-1)

    own_right = right_place * right_local
    col_sizes = lax.dynamic_slice_in_dim(right_sizes, own_right, right_local)
    col_starts = lax.dynamic_slice_in_dim(column_offset, own_right, right_local)
    col_index = spread(col_starts, col_sizes)
    col_select = one_hot(col_index, cap_col)
    pair_starts = lax.dynamic_slice_in_dim(pair_offset, left_place * left_local, left_local)
    local_index = spread(exclusive(own_sizes), own_sizes)
    pair_index = spread(pair_starts, own_sizes)

    def compact_right(tie):
        starts, tiles = after((col_starts, right_tiles), tie)
        return pl.pallas_call(
            compact_kernel,
            out_shape=jax.ShapeDtypeStruct((terms * right_b, cap_col, tile), BF16),
            grid_spec=pltpu.PrefetchScalarGridSpec(
                num_scalar_prefetch=1,
                grid=(terms, right_b),
                in_specs=[pl.BlockSpec((1, right_local, 1, tile, tile), lambda k, b, *_: (k, 0, b, 0, 0))],
                out_specs=pl.BlockSpec((1, cap_col, tile), lambda k, b, *_: (k * right_b + b, 0, 0)),
                scratch_shapes=[pltpu.VMEM((cap_col + tile, tile), F32)],
            ),
            cost_estimate=cost(1e6, 1e5),
        )(starts, tiles)

    with jax.named_scope("pack"):
        other = lax.dynamic_index_in_dim(wavefunction, 1 - side, 0, keepdims=False)
        other_rows = matmul(one_hot(local_index, cap_row).T, other).astype(BF16)
        incoming = []
        for n in range(2):
            outgoing = matmul(other_rows, col_select[:, bounds[n] : bounds[n + 1]]).astype(BF16)
            incoming.append(lax.ppermute(outgoing, "lsec", swap_side))
        compact = compact_right(outgoing)
        mine = lax.dynamic_index_in_dim(after(wavefunction, compact), side, 0, keepdims=False)
        mine_rows = matmul(one_hot(pair_index, cap_pair).T, mine).astype(BF16)
        pair_total = jnp.sum(lax.dynamic_index_in_dim(pair_sizes, place, 0, keepdims=False))
        partner_base = jnp.where(side == 0, own_count, 0)
        partner_count = pair_total - own_count
        spots = jnp.arange(cap_row, dtype=I32)
        partner_select = one_hot(jnp.where(spots < partner_count, partner_base + spots, -1), cap_pair).T
        pair = []
        for n in range(2):
            own_part = matmul(mine_rows, col_select[:, bounds[n] : bounds[n + 1]])
            pair.append((own_part + matmul(partner_select, incoming[n])).astype(BF16))

    upward = [[part] for part in pair]
    downward = [[part] for part in pair]
    hops = []

    def hop(n, *ties):
        up, down = after((upward[n][-1], downward[n][-1]), *ties)
        with jax.named_scope("chain"):
            upward[n].append(lax.ppermute(up, "lsec", [(i, i + 2) for i in range(left_devices - 2)]))
            downward[n].append(lax.ppermute(down, "lsec", [(i + 2, i) for i in range(left_devices - 2)]))
        hops.append((upward[n][-1], downward[n][-1]))

    def tall_permute(value, d):
        with jax.named_scope("right_exchange"):
            return lax.ppermute(
                value, "rsec", [(i, ((i // 2 - d) % height) * 2 + i % 2) for i in range(right_devices)]
            )

    def core_permute(value):
        with jax.named_scope("right_exchange"):
            return lax.ppermute(value, "rsec", swap_core)

    def prepare_left(tie):
        with jax.named_scope("left_exchange"):
            own_weight = lax.dynamic_slice_in_dim(left_weight, left_place * left_local, left_local, 1)
            left_scaled = (after(left_tiles, incoming[1]).astype(F32) * own_weight[..., None, None]).astype(BF16)
            left_other = lax.ppermute(left_scaled, "lsec", swap_side)
            left_scaled, left_other = after((left_scaled, left_other), tie)
            left_pair = jnp.where(
                side == 0, jnp.concatenate([left_scaled, left_other], 1), jnp.concatenate([left_other, left_scaled], 1)
            )
            source = lax.dynamic_slice_in_dim(left_source, place * 2 * left_local, 2 * left_local, 1)
            source = jnp.transpose(source, (1, 0, 2))
            source_offset = lookup(pair_offset, source)
            left_slot = source // (2 * left_local)
            left_start = jnp.minimum(source_offset // 16 * 16, cap_pair - WIN)
            source_size = lookup(left_sizes, source)
            moved = jnp.where(
                offsets < source_size[..., None], (source_offset - left_start)[..., None] + offsets, -1
            )
            left_shifted = jnp.einsum(
                "klbij,lkbjc->lkbic", left_pair, one_hot(moved, WIN), preferred_element_type=F32
            ).astype(BF16).reshape(2 * left_local * terms, left_b, tile, WIN)
        return left_slot, left_start, left_shifted

    def make_lists(tie):
        with jax.named_scope("lists"):
            both = after(listed, tie)
            both = jnp.transpose(jnp.stack(both), (1, 0, 3, 2, 4))
            slots = jnp.arange(right_devices, dtype=I32)
            groups = 2 * ((tall + slots // 2) % height) + (core + slots) % 2
            ordered = both[0].reshape(-1).astype(I32)
            weights = both[1].reshape(-1)
            items = ordered.shape[0]
            number = jnp.arange(items, dtype=I32)
            key = jnp.where(ordered // right_local == right_place, number, items + number)
            key, ordered, weights = lax.sort((key, ordered, weights), num_keys=1)
            active = key < items
            number = key % items
            item_slot = number // (right_local * per_sector)
            sector = (2 * ((tall + item_slot // 2) % height) + (core + item_slot) % 2) * right_local
            sector = sector + number // per_sector % right_local
            low = lookup(column_offset, sector)
            high = low + lookup(right_sizes, sector)
            from_offset = lookup(column_offset, ordered)
            window = jnp.minimum(from_offset // 128 * 128, cap_col - WIN)
            edges = jnp.arange(panels, dtype=I32) * WIN
            earlier = item_slot[None, None, :] < slots[:, None, None]
            same = item_slot[None, None, :] == slots[:, None, None]
            before = active & (earlier | (same & (high <= edges[None, :, None])))
            within = active & (earlier | (same & (low < edges[None, :, None] + WIN)))
            panel_first = jnp.sum(before.astype(I32), -1)
            panel_last = jnp.sum(within.astype(I32), -1)
            fields = (number % per_sector, low, high, window, from_offset - window, lookup(right_sizes, ordered), weights)
        return fields, panel_first, panel_last

    per_sector = terms * right_b
    panels = (cap_col + WIN - 1) // WIN
    rows = 2 * cap_half
    halves = lax.dynamic_slice_in_dim(half_offset, place * 2, 2, 0) + jnp.arange(2, dtype=I32)[:, None] * cap_half
    anywhere = pl.BlockSpec(memory_space=pl.ANY)

    def build(parts, d, lists, tie):
        fields, panel_first, panel_last = lists
        chosen = slice(2 * d, 2 * d + 2)
        scalars = (*fields, panel_first[chosen].reshape(-1), panel_last[chosen].reshape(-1))
        split = len(parts[0])
        inputs = after(parts[0] + parts[1], tie)
        specs = []
        for slot in range(2):
            for part in parts[slot]:
                specs.append(
                    pl.BlockSpec(
                        (part.shape[0], WIN, tile),
                        lambda s, p, *_, slot=slot: (0, jnp.where(s == slot, p, (panels - 1) * (1 - slot)), 0),
                    )
                )
        with jax.named_scope("build"):
            return pl.pallas_call(
                functools.partial(build_kernel, (widths, right_b, panels, split, fields[0].shape[0])),
                out_shape=[jax.ShapeDtypeStruct((terms * width, 2 * panels * WIN), BF16) for width in widths],
                grid_spec=pltpu.PrefetchScalarGridSpec(
                    num_scalar_prefetch=len(scalars),
                    grid=(2, panels),
                    in_specs=specs,
                    out_specs=[
                        pl.BlockSpec((terms * width, WIN), lambda s, p, *_: (0, s * panels + p)) for width in widths
                    ],
                    scratch_shapes=[pltpu.VMEM((per_sector, WIN, tile), BF16)],
                ),
                compiler_params=pltpu.CompilerParams(vmem_limit_bytes=VMEM_LIMIT),
                cost_estimate=cost(1e6, 1e5),
            )(*scalars, *inputs)

    def apply_left(n, left_parts):
        left_slot, left_start, left_shifted = left_parts
        blocks = upward[n] + downward[n][1:]
        scalars = (place.reshape(1), left_slot.reshape(-1), left_start.reshape(-1), halves.reshape(-1))
        width = widths[n]
        with jax.named_scope("apply_left"):
            return pl.pallas_call(
                functools.partial(left_kernel, (chain, terms, 2 * left_local, width)),
                out_shape=jax.ShapeDtypeStruct((rows + tile, terms * width), BF16),
                grid_spec=pltpu.PrefetchScalarGridSpec(
                    num_scalar_prefetch=len(scalars),
                    grid=(1,),
                    in_specs=[anywhere] * (len(blocks) + 1),
                    out_specs=pl.BlockSpec((rows + tile, terms * width), lambda i, *_: (0, 0)),
                    scratch_shapes=[
                        pltpu.VMEM((chain, cap_pair, width), BF16),
                        pltpu.VMEM((2 * left_local * terms, left_b, tile, WIN), BF16),
                        pltpu.SemaphoreType.DMA((2 * chain,)),
                    ],
                ),
                compiler_params=pltpu.CompilerParams(vmem_limit_bytes=VMEM_LIMIT),
                cost_estimate=cost(1e6, 1e5),
            )(*scalars, *blocks, left_shifted)

    own_list = jnp.stack([right_source.astype(F32), right_weight])
    listed = []
    for d in range(height):
        listed.append(tall_permute(own_list, d) if d else own_list)
        listed.append(core_permute(listed[-1]))
    near = core_permute(compact)
    far = [[[], []] for _ in range(1, height)]
    sent = []
    for term in range(terms):
        piece = compact[term * right_b : (term + 1) * right_b]
        if sent:
            piece = after(piece, sent[-1])
        for d in range(1, height):
            far[d - 1][0].append(tall_permute(piece, d))
        sent.append([far[d - 1][0][-1] for d in range(1, height)])

    hop(0, sent[0])
    hop(1, sent[1])
    lists = make_lists(pair[1])
    hop(0, near, lists, sent[2])
    built = [build([[compact], [near]], 0, lists, hops[0])]
    for d in range(1, height):
        far[d - 1][1] = [core_permute(piece) for piece in far[d - 1][0]]
    hop(1, built, sent[3])
    for d in range(1, height):
        built.append(build(far[d - 1], d, lists, hops[1]))
    for step in range(3, chain):
        hop(0, built if step == 3 else [])
        if step == 3:
            left_parts = prepare_left(hops[2])
            col_expand = jnp.arange(cap_col, dtype=I32)[:, None] == after(col_index, hops[2])[None, :]
            col_expand = after(col_expand.astype(BF16))
        hop(1, left_parts if step == 3 else [])
    product = apply_left(0, left_parts)
    span = panels * WIN

    with jax.named_scope("apply_right"):
        early = product[: 2 * cap_half]
        partial = [matmul(early, part[0]).astype(BF16) for part in built]
    product = apply_left(1, after(left_parts, partial))
    order = [1 - side, side]

    def finish(h, d, tie):
        with jax.named_scope("apply_right"):
            rows_late = lax.dynamic_slice_in_dim(after(product, tie), order[h] * cap_half, cap_half, 0)
            rows_early = lax.dynamic_slice_in_dim(partial[d], order[h] * cap_half, cap_half, 0)
            total = matmul(rows_late, built[d][1]) + rows_early.astype(F32)
            total = total.astype(BF16)
            return total[:, :cap_col], total[:, span : span + cap_col]

    begun = []

    def reduce_half(h):
        with jax.named_scope("reduce"):
            moved = []
            for d in list(range(1, height)) + [0]:
                stays, away = finish(h, d, begun[:h])
                summed = stays.astype(F32) + lax.ppermute(away, "rsec", swap_core).astype(F32)
                begun.append(summed)
                if d == 0:
                    moved.append(summed)
                else:
                    moved.append(
                        lax.ppermute(
                            summed.astype(BF16),
                            "rsec",
                            [(i, ((i // 2 + d) % height) * 2 + i % 2) for i in range(right_devices)],
                        ).astype(F32)
                    )
            return functools.reduce(jnp.add, moved[::-1]).astype(BF16)

    given = reduce_half(0)
    with jax.named_scope("reduce"):
        taken = lax.ppermute(given, "lsec", swap_side)
    kept = reduce_half(1)

    with jax.named_scope("unpack"):
        own_half = lax.dynamic_index_in_dim(half_offset, left_place, 0, keepdims=False)
        row_select = one_hot(spread(own_half, own_sizes), cap_half)

        both = jnp.stack([jnp.where(side == 0, kept, taken), jnp.where(side == 0, taken, kept)])
        both = jnp.einsum("rh,vhc->vrc", row_select, both, preferred_element_type=F32).astype(BF16)
        return jnp.einsum("vrc,cw->vrw", both, col_expand, preferred_element_type=F32).astype(BF16)


def local(wavefunction, left_tiles, left_source, left_weight, left_sizes, right_tiles, right_source, right_weight, right_sizes):
    _, rows_local, cols_local = wavefunction.shape
    left_devices = lax.axis_size("lsec")
    right_devices = lax.axis_size("rsec")

    def most(sizes, parts):
        here = jnp.arange(sizes.shape[0], dtype=I32) // (sizes.shape[0] // parts)
        return jnp.max(jnp.sum(jnp.where(here == jnp.arange(parts, dtype=I32)[:, None], sizes, 0), -1))

    most_rows = most(left_sizes, left_devices)
    most_half = most((left_sizes + 15) // 16 * 16, left_devices)
    most_pair = most(left_sizes, left_devices // 2)
    most_cols = most(right_sizes, right_devices)
    arguments = (wavefunction, left_tiles, left_source, left_weight, left_sizes, right_tiles, right_source, right_weight, right_sizes)
    branches = [general]
    choice = jnp.zeros((), I32)
    for level, (row, pair, half, col) in enumerate(LEVELS):
        caps = (
            rows_local * row // 16,
            rows_local * pair // 16,
            rows_local * half // 16,
            cols_local * col // 16 // 128 * 128,
        )
        fits = (most_rows <= caps[0]) & (most_pair <= caps[1]) & (most_half <= caps[2]) & (most_cols <= caps[3])
        branches.append(functools.partial(fast, caps))
        choice = jnp.where(fits, level + 1, choice)
    return lax.switch(choice, branches, *arguments)


LEVELS = ((16, 24, 16, 12), (14, 22, 14, 11), (12, 20, 12, 10))


def solution(mesh):
    return jax.shard_map(
        local,
        mesh=mesh,
        in_specs=(
            P(None, "lsec", "rsec"),
            P(None, "lsec", None, None, None),
            P(),
            P(),
            P(),
            P(None, "rsec", None, None, None),
            P(None, "rsec", None),
            P(None, "rsec", None),
            P(),
        ),
        out_specs=P(None, "lsec", "rsec"),
        check_vma=False,
    )
```

```python
import functools

import jax
import jax.numpy as jnp
from jax import lax
from jax.experimental import pallas as pl
from jax.experimental.pallas import tpu as pltpu
from jax.sharding import PartitionSpec as P

F32 = jnp.float32
BF16 = jnp.bfloat16
I32 = jnp.int32
WIN = 256
VMEM_LIMIT = 60 * 1024 * 1024


def sector_mask(sizes, tile):
    offsets = jnp.arange(tile, dtype=jnp.int32)
    return (offsets[None, :] < sizes[:, None]).reshape(-1)


def scaled_tiles(tiles, weight):
    return (tiles.astype(jnp.float32) * weight[..., None, None]).astype(jnp.bfloat16)


def weighted_right(selected_rows, scaled):
    return jnp.einsum("vlqbs,qbts->vlqt", selected_rows, scaled, preferred_element_type=jnp.float32)


def left_rows(arranged, product_fragments, source, weight):
    total = None
    for term in range(product_fragments.shape[0]):
        selected_rows = jnp.take(arranged[:, :, :, term, :], source[term], axis=1)
        scaled = scaled_tiles(product_fragments[term], weight[term])
        part = jnp.einsum(
            "mbij,vmbjc->vmic", scaled, selected_rows, preferred_element_type=jnp.float32
        )
        total = part if total is None else total + part
    return total.reshape(total.shape[0], -1, total.shape[-1])


def general(
    wavefunction,
    left_tiles,
    left_source_sector,
    left_weight,
    left_sizes,
    right_tiles,
    right_source,
    right_weight,
    right_sizes,
):
    vectors, rows_local, cols_local = wavefunction.shape
    terms_count = right_tiles.shape[0]
    tile = right_tiles.shape[3]
    left_count = left_sizes.shape[0]
    right_count = right_sizes.shape[0]
    left_local = rows_local // tile
    right_local = cols_local // tile
    left_devices = lax.axis_size("lsec")
    width = cols_local // left_devices
    left_place = lax.axis_index("lsec")
    right_place = lax.axis_index("rsec")
    row_keep_mask = sector_mask(
        lax.dynamic_slice_in_dim(left_sizes, left_place * left_local, left_local), tile
    )
    col_keep = sector_mask(
        lax.dynamic_slice_in_dim(right_sizes, right_place * right_local, right_local), tile
    )
    masked = jnp.where(
        row_keep_mask[None, :, None] & col_keep[None, None, :],
        wavefunction,
        jnp.zeros((), wavefunction.dtype),
    )
    right_scaled = scaled_tiles(right_tiles, right_weight)
    gathered = lax.all_gather(masked, "rsec", axis=2, tiled=True)
    sector_block_list = gathered.reshape(vectors, rows_local, right_count, tile)
    products = []
    for term in range(terms_count):
        selected_rows = jnp.take(sector_block_list, right_source[term], axis=2)
        products.append(weighted_right(selected_rows, right_scaled[term]))
    rounded = [
        item.astype(jnp.bfloat16).reshape(vectors, rows_local, left_devices, width)
        for item in products
    ]
    outgoing = jnp.stack(rounded, axis=3)
    exchanged_values = lax.all_to_all(
        outgoing.reshape(vectors, rows_local, -1), "lsec", split_axis=2, concat_axis=1, tiled=True
    )
    arranged = exchanged_values.reshape(vectors, left_count, tile, terms_count, width)
    sigma_part = left_rows(
        arranged,
        lax.all_gather(left_tiles, "lsec", axis=1, tiled=True),
        left_source_sector,
        left_weight,
    )
    row_all = sector_mask(left_sizes, tile)
    columns = right_place * cols_local + left_place * width + jnp.arange(width, dtype=jnp.int32)
    column_sizes = jnp.take(right_sizes, columns // tile)
    column_keep = columns % tile < column_sizes
    result = jnp.where(
        row_all[None, :, None] & column_keep[None, None, :],
        sigma_part,
        jnp.zeros((), sigma_part.dtype),
    )
    return lax.all_to_all(
        result.astype(jnp.bfloat16), "lsec", split_axis=1, concat_axis=2, tiled=True
    )


def exclusive(values):
    return jnp.cumsum(values, axis=-1) - values


def one_hot(index, count):
    return (index[..., None] == jnp.arange(count, dtype=I32)).astype(BF16)


def lookup(table, index):
    return jnp.sum(jnp.where(index[..., None] == jnp.arange(table.shape[0], dtype=I32), table, 0), axis=-1)


def matmul(a, b):
    return jnp.matmul(a, b, preferred_element_type=F32)


def after(value, *others):
    return lax.optimization_barrier((value, others))[0]


def cost(flops, bytes_accessed):
    return pl.CostEstimate(flops=int(flops), bytes_accessed=int(bytes_accessed), transcendentals=0)


def compact_kernel(start_ref, tiles_ref, out_ref, rows_ref):
    tile = tiles_ref.shape[3]

    @pl.when((pl.program_id(0) == 0) & (pl.program_id(1) == 0))
    def _():
        rows_ref[...] = jnp.zeros_like(rows_ref)

    for q in range(tiles_ref.shape[1]):
        rows_ref[pl.ds(start_ref[q], tile), :] = tiles_ref[0, q, 0].astype(F32)
    out_ref[0] = rows_ref[: out_ref.shape[1], :].astype(BF16)


def build_kernel(dims, item_kb, item_lo, item_hi, item_win, item_shift, item_size, item_weight, panel_first, panel_last, *refs):
    widths, right_b, panels, split, items = dims
    outs = refs[-1 - len(widths) : -1]
    held = refs[-1]
    parts = refs[: -1 - len(widths)]
    tile = held.shape[2]
    here = pl.program_id(0) * panels + pl.program_id(1)
    for slot in range(2):
        @pl.when(pl.program_id(0) == slot)
        def _(slot=slot):
            base = 0
            for part in parts[slot * split : (slot + 1) * split]:
                held[base : base + part.shape[0]] = part[...]
                base += part.shape[0]

    for out in outs:
        out[...] = jnp.zeros_like(out)
    column = lax.broadcasted_iota(I32, (WIN, tile), 0) + pl.program_id(1) * WIN
    source = lax.broadcasted_iota(I32, (WIN, tile), 1)
    target = lax.broadcasted_iota(I32, (WIN, tile), 0) - source
    first = panel_first[here]
    last = panel_last[here]

    def step(g, carry):
        values = []
        for u in range(2):
            raw = first + 2 * g + u
            it = jnp.minimum(raw, items - 1)
            kb = item_kb[it]
            block = (held[kb].astype(F32) * item_weight[it])
            block = jnp.where((column >= item_lo[it]) & (column < item_hi[it]), block, 0.0).astype(BF16)
            size = jnp.where(raw < last, item_size[it], 0)
            shift = jnp.where((target == item_shift[it]) & (source < size), 1.0, 0.0).astype(BF16)
            value = lax.dot_general(shift, block, (((1,), (1,)), ((), ())), preferred_element_type=F32)
            values.append((kb // right_b, item_win[it], value.astype(BF16)))
        for term, window, value in values:
            for part in range(WIN // tile):
                start = window + part * tile
                base = 0
                for out, width in zip(outs, widths):
                    @pl.when((start >= base) & (start < base + width))
                    def _(out=out, width=width, base=base, part=part, term=term, start=start, value=value):
                        row = jnp.clip(term * width + start - base, 0, out.shape[0] - tile)
                        row = pl.multiple_of(row, tile)
                        out[pl.ds(row, tile), :] += value[part * tile : (part + 1) * tile]
                    base += width
        return carry

    lax.fori_loop(0, (last - first + 1) // 2, step, 0)


def left_kernel(dims, place_ref, left_slot, left_start, row_start, *refs):
    chain, terms, steps, width = dims
    blocks = refs[: 2 * chain - 1]
    left_ref, out_ref, gathered, left_tiles, sem = refs[2 * chain - 1 :]
    tile = left_ref.shape[2]
    place = place_ref[0]

    def each(action):
        action(pltpu.make_async_copy(blocks[0], gathered.at[place], sem.at[0]))
        for d in range(1, chain):
            @pl.when(place - d >= 0)
            def _():
                action(pltpu.make_async_copy(blocks[d], gathered.at[jnp.maximum(place - d, 0)], sem.at[d]))

            @pl.when(place + d < chain)
            def _():
                action(
                    pltpu.make_async_copy(
                        blocks[chain - 1 + d], gathered.at[jnp.minimum(place + d, chain - 1)], sem.at[chain - 1 + d]
                    )
                )
        action(pltpu.make_async_copy(left_ref, left_tiles, sem.at[2 * chain - 1]))

    each(lambda copy: copy.start())
    out_ref[...] = jnp.zeros_like(out_ref)
    each(lambda copy: copy.wait())

    def sector_step(sector, carry):
        row = pl.multiple_of(row_start[sector], 16)
        for term in range(terms):
            i = sector * terms + term
            first_start = pl.multiple_of(left_start[2 * i], 16)
            second_start = pl.multiple_of(left_start[2 * i + 1], 16)
            for n in range(0, width, WIN):
                lanes = slice(n, min(n + WIN, width))
                value = jnp.dot(
                    left_tiles[i, 0],
                    gathered[left_slot[2 * i], pl.ds(first_start, WIN), lanes],
                    preferred_element_type=F32,
                ) + jnp.dot(
                    left_tiles[i, 1],
                    gathered[left_slot[2 * i + 1], pl.ds(second_start, WIN), lanes],
                    preferred_element_type=F32,
                )
                out_ref[pl.ds(row, tile), term * width + n : term * width + lanes.stop] = value.astype(BF16)
        return carry

    lax.fori_loop(0, steps, sector_step, 0)


def right_kernel(heights, halves, first_ref, rows_ref, cols_ref, left_ref, right_ref, *refs):
    out_ref = refs[-1]
    added = refs[:-1]
    full = out_ref.shape[0] // halves
    columns = cols_ref[pl.program_id(0)] - pl.program_id(1) * WIN

    @pl.when(columns <= 0)
    def _():
        out_ref[...] = jnp.zeros_like(out_ref)

    for half in range(halves):
        lower = 0
        for height in heights:
            count = rows_ref[half]

            @pl.when((columns > 0) & (count > lower) & (count <= height))
            def _(half=half, height=height):
                rows = slice(half * full, half * full + height)
                value = jnp.dot(left_ref[rows], right_ref[...], preferred_element_type=F32)
                for other in added:
                    value = value + other[rows].astype(F32)
                out_ref[rows] = value.astype(BF16)
                if height < full:
                    out_ref[half * full + height : (half + 1) * full] = jnp.zeros(
                        (full - height, out_ref.shape[1]), BF16
                    )

            lower = height


def unpack_kernel(group, row_start, row_size, col_start, col_shift, col_size, packed_ref, out_ref, select, rows):
    sectors, _, tile = select.shape

    @pl.when((pl.program_id(0) == 0) & (pl.program_id(1) == 0))
    def _():
        state = lax.broadcasted_iota(I32, (WIN, tile), 1)
        spot = lax.broadcasted_iota(I32, (WIN, tile), 0) - state
        for q in range(sectors):
            select[q] = jnp.where((spot == col_shift[q]) & (state < col_size[q]), 1.0, 0.0).astype(BF16)

    for u in range(group):
        sector = pl.program_id(1) * group + u
        start = pl.multiple_of(row_start[sector], 16)
        value = packed_ref[0, pl.ds(start, tile), :].astype(F32)
        keep = lax.broadcasted_iota(I32, value.shape, 0) < row_size[sector]
        rows[u * tile : (u + 1) * tile] = jnp.where(keep, value, 0.0).astype(BF16)
    for q in range(sectors):
        start = pl.multiple_of(col_start[q], 128)
        value = jnp.dot(rows[:, pl.ds(start, WIN)], select[q], preferred_element_type=F32)
        out_ref[0, :, q * tile : (q + 1) * tile] = value.astype(BF16)


def fast(caps, wavefunction, left_tiles, left_source, left_weight, left_sizes, right_tiles, right_source, right_weight, right_sizes):
    cap_row, cap_pair, cap_half, cap_col = caps
    vectors, rows_local, cols_local = wavefunction.shape
    terms, right_local, right_b, tile, _ = right_tiles.shape
    left_b = left_tiles.shape[2]
    left_devices = lax.axis_size("lsec")
    right_devices = lax.axis_size("rsec")
    left_local = rows_local // tile
    chain = left_devices // 2
    height = right_devices // 2
    left_place = lax.axis_index("lsec")
    right_place = lax.axis_index("rsec")
    side = left_place % 2
    place = left_place // 2
    core = right_place % 2
    tall = right_place // 2
    swap_side = [(i, i ^ 1) for i in range(left_devices)]
    swap_core = [(i, i ^ 1) for i in range(right_devices)]
    first_width = (cap_col // 128 + 1) // 2 * 128
    widths = [first_width, cap_col - first_width]
    bounds = [0, first_width, cap_col]

    own_sizes = lax.dynamic_slice_in_dim(left_sizes, left_place * left_local, left_local)
    pair_sizes = left_sizes.reshape(chain, 2 * left_local)
    pair_offset = exclusive(pair_sizes).reshape(-1)
    own_count = jnp.sum(own_sizes)
    rounded = (left_sizes + 15) // 16 * 16
    half_offset = exclusive(rounded.reshape(left_devices, left_local))
    half_count = jnp.sum(rounded.reshape(left_devices, left_local), axis=-1)
    column_offset = exclusive(right_sizes.reshape(right_devices, right_local)).reshape(-1)
    column_count = jnp.sum(right_sizes.reshape(right_devices, right_local), axis=-1)
    offsets = jnp.arange(tile, dtype=I32)

    def spread(starts, sizes):
        return jnp.where(offsets[None, :] < sizes[:, None], starts[:, None] + offsets[None, :], -1).reshape(-1)

    own_right = right_place * right_local
    col_sizes = lax.dynamic_slice_in_dim(right_sizes, own_right, right_local)
    col_starts = lax.dynamic_slice_in_dim(column_offset, own_right, right_local)
    col_index = spread(col_starts, col_sizes)
    col_select = one_hot(col_index, cap_col)
    pair_starts = lax.dynamic_slice_in_dim(pair_offset, left_place * left_local, left_local)
    local_index = spread(exclusive(own_sizes), own_sizes)
    pair_index = spread(pair_starts, own_sizes)

    def compact_right(tie):
        starts, tiles = after((col_starts, right_tiles), tie)
        return pl.pallas_call(
            compact_kernel,
            out_shape=jax.ShapeDtypeStruct((terms * right_b, cap_col, tile), BF16),
            grid_spec=pltpu.PrefetchScalarGridSpec(
                num_scalar_prefetch=1,
                grid=(terms, right_b),
                in_specs=[pl.BlockSpec((1, right_local, 1, tile, tile), lambda k, b, *_: (k, 0, b, 0, 0))],
                out_specs=pl.BlockSpec((1, cap_col, tile), lambda k, b, *_: (k * right_b + b, 0, 0)),
                scratch_shapes=[pltpu.VMEM((cap_col + tile, tile), F32)],
            ),
            cost_estimate=cost(1e6, 1e5),
        )(starts, tiles)

    with jax.named_scope("pack"):
        other = lax.dynamic_index_in_dim(wavefunction, 1 - side, 0, keepdims=False)
        other_rows = matmul(one_hot(local_index, cap_row).T, other).astype(BF16)
        incoming = []
        for n in range(2):
            outgoing = matmul(other_rows, col_select[:, bounds[n] : bounds[n + 1]]).astype(BF16)
            incoming.append(lax.ppermute(outgoing, "lsec", swap_side))
        compact = compact_right(outgoing)
        mine = lax.dynamic_index_in_dim(after(wavefunction, compact), side, 0, keepdims=False)
        mine_rows = matmul(one_hot(pair_index, cap_pair).T, mine).astype(BF16)
        pair_total = jnp.sum(lax.dynamic_index_in_dim(pair_sizes, place, 0, keepdims=False))
        partner_base = jnp.where(side == 0, own_count, 0)
        partner_count = pair_total - own_count
        spots = jnp.arange(cap_row, dtype=I32)
        partner_select = one_hot(jnp.where(spots < partner_count, partner_base + spots, -1), cap_pair).T
        pair = []
        for n in range(2):
            own_part = matmul(mine_rows, col_select[:, bounds[n] : bounds[n + 1]])
            pair.append((own_part + matmul(partner_select, incoming[n])).astype(BF16))

    upward = [[part] for part in pair]
    downward = [[part] for part in pair]
    hops = []

    def hop(n, *ties):
        up, down = after((upward[n][-1], downward[n][-1]), *ties)
        with jax.named_scope("chain"):
            upward[n].append(lax.ppermute(up, "lsec", [(i, i + 2) for i in range(left_devices - 2)]))
            downward[n].append(lax.ppermute(down, "lsec", [(i + 2, i) for i in range(left_devices - 2)]))
        hops.append((upward[n][-1], downward[n][-1]))

    def tall_permute(value, d):
        with jax.named_scope("right_exchange"):
            return lax.ppermute(
                value, "rsec", [(i, ((i // 2 - d) % height) * 2 + i % 2) for i in range(right_devices)]
            )

    def core_permute(value):
        with jax.named_scope("right_exchange"):
            return lax.ppermute(value, "rsec", swap_core)

    def prepare_left(tie):
        with jax.named_scope("left_exchange"):
            own_weight = lax.dynamic_slice_in_dim(left_weight, left_place * left_local, left_local, 1)
            left_scaled = (after(left_tiles, incoming[1]).astype(F32) * own_weight[..., None, None]).astype(BF16)
            left_other = lax.ppermute(left_scaled, "lsec", swap_side)
            left_scaled, left_other = after((left_scaled, left_other), tie)
            left_pair = jnp.where(
                side == 0, jnp.concatenate([left_scaled, left_other], 1), jnp.concatenate([left_other, left_scaled], 1)
            )
            source = lax.dynamic_slice_in_dim(left_source, place * 2 * left_local, 2 * left_local, 1)
            source = jnp.transpose(source, (1, 0, 2))
            source_offset = lookup(pair_offset, source)
            left_slot = source // (2 * left_local)
            left_start = jnp.minimum(source_offset // 16 * 16, cap_pair - WIN)
            source_size = lookup(left_sizes, source)
            moved = jnp.where(
                offsets < source_size[..., None], (source_offset - left_start)[..., None] + offsets, -1
            )
            left_shifted = jnp.einsum(
                "klbij,lkbjc->lkbic", left_pair, one_hot(moved, WIN), preferred_element_type=F32
            ).astype(BF16).reshape(2 * left_local * terms, left_b, tile, WIN)
        return left_slot, left_start, left_shifted

    def make_lists(tie):
        with jax.named_scope("lists"):
            both = after(listed, tie)
            both = jnp.transpose(jnp.stack(both), (1, 0, 3, 2, 4))
            slots = jnp.arange(right_devices, dtype=I32)
            groups = 2 * ((tall + slots // 2) % height) + (core + slots) % 2
            ordered = both[0].reshape(-1).astype(I32)
            weights = both[1].reshape(-1)
            items = ordered.shape[0]
            number = jnp.arange(items, dtype=I32)
            key = jnp.where(ordered // right_local == right_place, number, items + number)
            key, ordered, weights = lax.sort((key, ordered, weights), num_keys=1)
            active = key < items
            number = key % items
            item_slot = number // (right_local * per_sector)
            sector = (2 * ((tall + item_slot // 2) % height) + (core + item_slot) % 2) * right_local
            sector = sector + number // per_sector % right_local
            low = lookup(column_offset, sector)
            high = low + lookup(right_sizes, sector)
            from_offset = lookup(column_offset, ordered)
            window = jnp.minimum(from_offset // 128 * 128, cap_col - WIN)
            edges = jnp.arange(panels, dtype=I32) * WIN
            earlier = item_slot[None, None, :] < slots[:, None, None]
            same = item_slot[None, None, :] == slots[:, None, None]
            before = active & (earlier | (same & (high <= edges[None, :, None])))
            within = active & (earlier | (same & (low < edges[None, :, None] + WIN)))
            panel_first = jnp.sum(before.astype(I32), -1)
            panel_last = jnp.sum(within.astype(I32), -1)
            fields = (number % per_sector, low, high, window, from_offset - window, lookup(right_sizes, ordered), weights)
        return fields, panel_first, panel_last

    per_sector = terms * right_b
    panels = (cap_col + WIN - 1) // WIN
    rows = 2 * cap_half
    halves = lax.dynamic_slice_in_dim(half_offset, place * 2, 2, 0) + jnp.arange(2, dtype=I32)[:, None] * cap_half
    anywhere = pl.BlockSpec(memory_space=pl.ANY)

    def build(parts, d, lists, tie):
        fields, panel_first, panel_last = lists
        chosen = slice(2 * d, 2 * d + 2)
        scalars = (*fields, panel_first[chosen].reshape(-1), panel_last[chosen].reshape(-1))
        split = len(parts[0])
        inputs = after(parts[0] + parts[1], tie)
        specs = []
        for slot in range(2):
            for part in parts[slot]:
                specs.append(
                    pl.BlockSpec(
                        (part.shape[0], WIN, tile),
                        lambda s, p, *_, slot=slot: (0, jnp.where(s == slot, p, (panels - 1) * (1 - slot)), 0),
                    )
                )
        with jax.named_scope("build"):
            return pl.pallas_call(
                functools.partial(build_kernel, (widths, right_b, panels, split, fields[0].shape[0])),
                out_shape=[jax.ShapeDtypeStruct((terms * width, 2 * panels * WIN), BF16) for width in widths],
                grid_spec=pltpu.PrefetchScalarGridSpec(
                    num_scalar_prefetch=len(scalars),
                    grid=(2, panels),
                    in_specs=specs,
                    out_specs=[
                        pl.BlockSpec((terms * width, WIN), lambda s, p, *_: (0, s * panels + p)) for width in widths
                    ],
                    scratch_shapes=[pltpu.VMEM((per_sector, WIN, tile), BF16)],
                ),
                compiler_params=pltpu.CompilerParams(vmem_limit_bytes=VMEM_LIMIT),
                cost_estimate=cost(1e6, 1e5),
            )(*scalars, *inputs)

    def apply_left(n, left_parts):
        left_slot, left_start, left_shifted = left_parts
        blocks = upward[n] + downward[n][1:]
        scalars = (place.reshape(1), left_slot.reshape(-1), left_start.reshape(-1), halves.reshape(-1))
        width = widths[n]
        with jax.named_scope("apply_left"):
            return pl.pallas_call(
                functools.partial(left_kernel, (chain, terms, 2 * left_local, width)),
                out_shape=jax.ShapeDtypeStruct((rows + tile, terms * width), BF16),
                grid_spec=pltpu.PrefetchScalarGridSpec(
                    num_scalar_prefetch=len(scalars),
                    grid=(1,),
                    in_specs=[anywhere] * (len(blocks) + 1),
                    out_specs=pl.BlockSpec((rows + tile, terms * width), lambda i, *_: (0, 0)),
                    scratch_shapes=[
                        pltpu.VMEM((chain, cap_pair, width), BF16),
                        pltpu.VMEM((2 * left_local * terms, left_b, tile, WIN), BF16),
                        pltpu.SemaphoreType.DMA((2 * chain,)),
                    ],
                ),
                compiler_params=pltpu.CompilerParams(vmem_limit_bytes=VMEM_LIMIT),
                cost_estimate=cost(1e6, 1e5),
            )(*scalars, *blocks, left_shifted)

    own_list = jnp.stack([right_source.astype(F32), right_weight])
    listed = []
    for d in range(height):
        listed.append(tall_permute(own_list, d) if d else own_list)
        listed.append(core_permute(listed[-1]))
    near = core_permute(compact)
    far = [[[], []] for _ in range(1, height)]
    sent = []

    def send_far(*ties):
        term = len(sent)
        piece = after(compact[term * right_b : (term + 1) * right_b], *ties, *sent[-1:])
        for d in range(1, height):
            far[d - 1][0].append(tall_permute(piece, d))
        sent.append([far[d - 1][0][-1] for d in range(1, height)])

    send_far()
    hop(0)
    send_far(pair[0])
    hop(1, sent[0])
    send_far(pair[1])
    lists = make_lists(pair[1])
    built = [build([[compact], [near]], 0, lists, pair[1])]
    hop(0, built, sent[2:])
    for term in range(3, terms):
        send_far(built)
    for d in range(1, height):
        far[d - 1][1] = [core_permute(piece) for piece in far[d - 1][0]]
    hop(1, sent)
    for d in range(1, height):
        built.append(build(far[d - 1], d, lists, hops[1]))
    for step in range(3, chain):
        hop(0, built if step == 3 else [])
        if step == 3:
            left_parts = prepare_left(hops[2])
        hop(1, left_parts if step == 3 else [])
    product = apply_left(0, left_parts)
    span = panels * WIN
    heights = [h for h in range(640, cap_half, 128)] + [cap_half]
    half_rows = lax.dynamic_slice_in_dim(half_count, place * 2, 2, 0)

    def apply_right(left, right, slots, halves, first, row_counts, columns, added):
        width = left.shape[1]
        full = halves * cap_half
        number = columns.shape[0]
        block = pl.BlockSpec((full, WIN), lambda s, p, *_: (0, s * panels + p))
        scalars = (first.reshape(1), row_counts, columns)
        return pl.pallas_call(
            functools.partial(right_kernel, heights, halves),
            out_shape=jax.ShapeDtypeStruct((full, number * span), BF16),
            grid_spec=pltpu.PrefetchScalarGridSpec(
                num_scalar_prefetch=3,
                grid=(number, panels),
                in_specs=[
                    pl.BlockSpec((full, width), lambda s, p, first, *_: (first[0], 0)),
                    pl.BlockSpec((width, WIN), lambda s, p, *_: (0, (s + slots) * panels + p)),
                ]
                + (
                    [pl.BlockSpec((full, WIN), lambda s, p, first, *_: (first[0], (s + slots) * panels + p))]
                    if added
                    else []
                )
                + (
                    [pl.BlockSpec((full, WIN), lambda s, p, first, *_: (first[0], s * panels + p))]
                    if len(added) > 1
                    else []
                ),
                out_specs=block,
            ),
            compiler_params=pltpu.CompilerParams(vmem_limit_bytes=VMEM_LIMIT),
            cost_estimate=cost(1e6, 1e5),
        )(*scalars, left, right, *added)

    groups_of = [2 * ((tall + d) % height) for d in range(height)]
    slot_cols = [
        lookup(column_count, jnp.stack([groups_of[d] + core, groups_of[d] + 1 - core])) for d in range(height)
    ]
    zero = jnp.zeros((), I32)
    with jax.named_scope("apply_right"):
        partial = [
            apply_right(product, built[d][0], 0, 2, zero, half_rows, slot_cols[d], []) for d in range(height)
        ]
    product = apply_left(1, after(left_parts, partial))
    order = [1 - side, side]

    with jax.named_scope("apply_right"):
        backward = list(range(1, height)) + [0]
        crossed = {}
        last = product
        for d in backward:
            away = apply_right(
                after(product, last), built[d][1], 1, 2, zero, half_rows, slot_cols[d][1:], [partial[d]]
            )
            last = away
            with jax.named_scope("reduce"):
                crossed[d] = lax.ppermute(away, "rsec", swap_core)

        def stays(h, d, tie):
            return apply_right(
                after(product, tie),
                built[d][1],
                0,
                1,
                order[h],
                lax.dynamic_slice_in_dim(half_rows, order[h], 1),
                slot_cols[d][:1],
                [partial[d], crossed[d]],
            )

        arrived = [[], []]
        for d in range(1, height):
            for h in range(2):
                last = stays(h, d, last)
                with jax.named_scope("reduce"):
                    arrived[h].append(
                        lax.ppermute(
                            last, "rsec", [(i, ((i // 2 + d) % height) * 2 + i % 2) for i in range(right_devices)]
                        )
                    )
        results = []
        for h in range(2):
            last = stays(h, 0, last)
            total = last.astype(F32)
            for value in arrived[h]:
                total = total + value.astype(F32)
            results.append(total.astype(BF16))
    given, kept = results
    with jax.named_scope("reduce"):
        taken = lax.ppermute(given, "lsec", swap_side)

    with jax.named_scope("unpack"):
        both = jnp.stack([jnp.where(side == 0, kept, taken), jnp.where(side == 0, taken, kept)])
        both = jnp.pad(both, ((0, 0), (0, tile), (0, 0)))
        col_window = jnp.minimum(col_starts // 128 * 128, cap_col - WIN)
        group = 4 if left_local % 4 == 0 else 1
        scalars = (
            lax.dynamic_index_in_dim(half_offset, left_place, 0, keepdims=False),
            own_sizes,
            col_window,
            col_starts - col_window,
            col_sizes,
        )
        return pl.pallas_call(
            functools.partial(unpack_kernel, group),
            out_shape=jax.ShapeDtypeStruct((vectors, rows_local, cols_local), BF16),
            grid_spec=pltpu.PrefetchScalarGridSpec(
                num_scalar_prefetch=len(scalars),
                grid=(vectors, left_local // group),
                in_specs=[pl.BlockSpec((1, cap_half + tile, span), lambda v, r, *_: (v, 0, 0))],
                out_specs=pl.BlockSpec((1, group * tile, cols_local), lambda v, r, *_: (v, r, 0)),
                scratch_shapes=[
                    pltpu.VMEM((right_local, WIN, tile), BF16),
                    pltpu.VMEM((group * tile, span), BF16),
                ],
            ),
            compiler_params=pltpu.CompilerParams(vmem_limit_bytes=VMEM_LIMIT),
        )(*scalars, both)


def local(wavefunction, left_tiles, left_source, left_weight, left_sizes, right_tiles, right_source, right_weight, right_sizes):
    _, rows_local, cols_local = wavefunction.shape
    left_devices = lax.axis_size("lsec")
    right_devices = lax.axis_size("rsec")

    def most(sizes, parts):
        here = jnp.arange(sizes.shape[0], dtype=I32) // (sizes.shape[0] // parts)
        return jnp.max(jnp.sum(jnp.where(here == jnp.arange(parts, dtype=I32)[:, None], sizes, 0), -1))

    most_rows = most(left_sizes, left_devices)
    most_half = most((left_sizes + 15) // 16 * 16, left_devices)
    most_pair = most(left_sizes, left_devices // 2)
    most_cols = most(right_sizes, right_devices)
    arguments = (wavefunction, left_tiles, left_source, left_weight, left_sizes, right_tiles, right_source, right_weight, right_sizes)
    branches = [general]
    choice = jnp.zeros((), I32)
    for level, (row, pair, half, col) in enumerate(LEVELS):
        caps = (
            rows_local * row // 16,
            rows_local * pair // 16,
            rows_local * half // 16,
            cols_local * col // 16 // 128 * 128,
        )
        fits = (most_rows <= caps[0]) & (most_pair <= caps[1]) & (most_half <= caps[2]) & (most_cols <= caps[3])
        branches.append(functools.partial(fast, caps))
        choice = jnp.where(fits, level + 1, choice)
    return lax.switch(choice, branches, *arguments)


LEVELS = ((16, 24, 16, 12), (14, 22, 14, 11), (12, 20, 12, 10))


def solution(mesh):
    return jax.shard_map(
        local,
        mesh=mesh,
        in_specs=(
            P(None, "lsec", "rsec"),
            P(None, "lsec", None, None, None),
            P(),
            P(),
            P(),
            P(None, "rsec", None, None, None),
            P(None, "rsec", None),
            P(None, "rsec", None),
            P(),
        ),
        out_specs=P(None, "lsec", "rsec"),
        check_vma=False,
    )
```

```python
import functools

import jax
import jax.numpy as jnp
from jax import lax
from jax.experimental import pallas as pl
from jax.experimental.pallas import tpu as pltpu
from jax.sharding import PartitionSpec as P

F32 = jnp.float32
BF16 = jnp.bfloat16
I32 = jnp.int32
WIN = 256
VMEM_LIMIT = 60 * 1024 * 1024


def sector_mask(sizes, tile):
    offsets = jnp.arange(tile, dtype=jnp.int32)
    return (offsets[None, :] < sizes[:, None]).reshape(-1)


def scaled_tiles(tiles, weight):
    return (tiles.astype(jnp.float32) * weight[..., None, None]).astype(jnp.bfloat16)


def weighted_right(selected_rows, scaled):
    return jnp.einsum("vlqbs,qbts->vlqt", selected_rows, scaled, preferred_element_type=jnp.float32)


def left_rows(arranged, product_fragments, source, weight):
    total = None
    for term in range(product_fragments.shape[0]):
        selected_rows = jnp.take(arranged[:, :, :, term, :], source[term], axis=1)
        scaled = scaled_tiles(product_fragments[term], weight[term])
        part = jnp.einsum(
            "mbij,vmbjc->vmic", scaled, selected_rows, preferred_element_type=jnp.float32
        )
        total = part if total is None else total + part
    return total.reshape(total.shape[0], -1, total.shape[-1])


def general(
    wavefunction,
    left_tiles,
    left_source_sector,
    left_weight,
    left_sizes,
    right_tiles,
    right_source,
    right_weight,
    right_sizes,
):
    vectors, rows_local, cols_local = wavefunction.shape
    terms_count = right_tiles.shape[0]
    tile = right_tiles.shape[3]
    left_count = left_sizes.shape[0]
    right_count = right_sizes.shape[0]
    left_local = rows_local // tile
    right_local = cols_local // tile
    left_devices = lax.axis_size("lsec")
    width = cols_local // left_devices
    left_place = lax.axis_index("lsec")
    right_place = lax.axis_index("rsec")
    row_keep_mask = sector_mask(
        lax.dynamic_slice_in_dim(left_sizes, left_place * left_local, left_local), tile
    )
    col_keep = sector_mask(
        lax.dynamic_slice_in_dim(right_sizes, right_place * right_local, right_local), tile
    )
    masked = jnp.where(
        row_keep_mask[None, :, None] & col_keep[None, None, :],
        wavefunction,
        jnp.zeros((), wavefunction.dtype),
    )
    right_scaled = scaled_tiles(right_tiles, right_weight)
    gathered = lax.all_gather(masked, "rsec", axis=2, tiled=True)
    sector_block_list = gathered.reshape(vectors, rows_local, right_count, tile)
    products = []
    for term in range(terms_count):
        selected_rows = jnp.take(sector_block_list, right_source[term], axis=2)
        products.append(weighted_right(selected_rows, right_scaled[term]))
    rounded = [
        item.astype(jnp.bfloat16).reshape(vectors, rows_local, left_devices, width)
        for item in products
    ]
    outgoing = jnp.stack(rounded, axis=3)
    exchanged_values = lax.all_to_all(
        outgoing.reshape(vectors, rows_local, -1), "lsec", split_axis=2, concat_axis=1, tiled=True
    )
    arranged = exchanged_values.reshape(vectors, left_count, tile, terms_count, width)
    sigma_part = left_rows(
        arranged,
        lax.all_gather(left_tiles, "lsec", axis=1, tiled=True),
        left_source_sector,
        left_weight,
    )
    row_all = sector_mask(left_sizes, tile)
    columns = right_place * cols_local + left_place * width + jnp.arange(width, dtype=jnp.int32)
    column_sizes = jnp.take(right_sizes, columns // tile)
    column_keep = columns % tile < column_sizes
    result = jnp.where(
        row_all[None, :, None] & column_keep[None, None, :],
        sigma_part,
        jnp.zeros((), sigma_part.dtype),
    )
    return lax.all_to_all(
        result.astype(jnp.bfloat16), "lsec", split_axis=1, concat_axis=2, tiled=True
    )


def exclusive(values):
    return jnp.cumsum(values, axis=-1) - values


def one_hot(index, count):
    return (index[..., None] == jnp.arange(count, dtype=I32)).astype(BF16)


def lookup(table, index):
    return jnp.sum(jnp.where(index[..., None] == jnp.arange(table.shape[0], dtype=I32), table, 0), axis=-1)


def matmul(a, b):
    return jnp.matmul(a, b, preferred_element_type=F32)


def after(value, *others):
    return lax.optimization_barrier((value, others))[0]


def cost(flops, bytes_accessed):
    return pl.CostEstimate(flops=int(flops), bytes_accessed=int(bytes_accessed), transcendentals=0)


def compact_kernel(start_ref, tiles_ref, out_ref, rows_ref):
    tile = tiles_ref.shape[3]

    @pl.when((pl.program_id(0) == 0) & (pl.program_id(1) == 0))
    def _():
        rows_ref[...] = jnp.zeros_like(rows_ref)

    for q in range(tiles_ref.shape[1]):
        rows_ref[pl.ds(start_ref[q], tile), :] = tiles_ref[0, q, 0].astype(F32)
    out_ref[0] = rows_ref[: out_ref.shape[1], :].astype(BF16)


def build_kernel(dims, item_kb, item_lo, item_hi, item_win, item_shift, item_size, item_weight, panel_first, panel_last, *refs):
    widths, right_b, panels, split, items = dims
    outs = refs[-1 - len(widths) : -1]
    held = refs[-1]
    parts = refs[: -1 - len(widths)]
    tile = held.shape[2]
    here = pl.program_id(0) * panels + pl.program_id(1)
    for slot in range(2):
        @pl.when(pl.program_id(0) == slot)
        def _(slot=slot):
            base = 0
            for part in parts[slot * split : (slot + 1) * split]:
                held[base : base + part.shape[0]] = part[...]
                base += part.shape[0]

    for out in outs:
        out[...] = jnp.zeros_like(out)
    column = lax.broadcasted_iota(I32, (WIN, tile), 0) + pl.program_id(1) * WIN
    source = lax.broadcasted_iota(I32, (WIN, tile), 1)
    target = lax.broadcasted_iota(I32, (WIN, tile), 0) - source
    first = panel_first[here]
    last = panel_last[here]

    def step(g, carry):
        values = []
        for u in range(2):
            raw = first + 2 * g + u
            it = jnp.minimum(raw, items - 1)
            kb = item_kb[it]
            block = (held[kb].astype(F32) * item_weight[it])
            block = jnp.where((column >= item_lo[it]) & (column < item_hi[it]), block, 0.0).astype(BF16)
            size = jnp.where(raw < last, item_size[it], 0)
            shift = jnp.where((target == item_shift[it]) & (source < size), 1.0, 0.0).astype(BF16)
            value = lax.dot_general(shift, block, (((1,), (1,)), ((), ())), preferred_element_type=F32)
            values.append((kb // right_b, item_win[it], value.astype(BF16)))
        for term, window, value in values:
            for part in range(WIN // tile):
                start = window + part * tile
                base = 0
                for out, width in zip(outs, widths):
                    @pl.when((start >= base) & (start < base + width))
                    def _(out=out, width=width, base=base, part=part, term=term, start=start, value=value):
                        row = jnp.clip(term * width + start - base, 0, out.shape[0] - tile)
                        row = pl.multiple_of(row, tile)
                        out[pl.ds(row, tile), :] += value[part * tile : (part + 1) * tile]
                    base += width
        return carry

    lax.fori_loop(0, (last - first + 1) // 2, step, 0)


def left_kernel(dims, place_ref, left_slot, left_start, row_start, *refs):
    chain, terms, steps, width = dims
    blocks = refs[: 2 * chain - 1]
    left_ref, out_ref, gathered, left_tiles, sem = refs[2 * chain - 1 :]
    tile = left_ref.shape[2]
    place = place_ref[0]

    def each(action):
        action(pltpu.make_async_copy(blocks[0], gathered.at[place], sem.at[0]))
        for d in range(1, chain):
            @pl.when(place - d >= 0)
            def _():
                action(pltpu.make_async_copy(blocks[d], gathered.at[jnp.maximum(place - d, 0)], sem.at[d]))

            @pl.when(place + d < chain)
            def _():
                action(
                    pltpu.make_async_copy(
                        blocks[chain - 1 + d], gathered.at[jnp.minimum(place + d, chain - 1)], sem.at[chain - 1 + d]
                    )
                )
        action(pltpu.make_async_copy(left_ref, left_tiles, sem.at[2 * chain - 1]))

    each(lambda copy: copy.start())
    out_ref[...] = jnp.zeros_like(out_ref)
    each(lambda copy: copy.wait())

    def sector_step(sector, carry):
        row = pl.multiple_of(row_start[sector], 16)
        for term in range(terms):
            i = sector * terms + term
            first_start = pl.multiple_of(left_start[2 * i], 16)
            second_start = pl.multiple_of(left_start[2 * i + 1], 16)
            for n in range(0, width, WIN):
                lanes = slice(n, min(n + WIN, width))
                value = jnp.dot(
                    left_tiles[i, 0],
                    gathered[left_slot[2 * i], pl.ds(first_start, WIN), lanes],
                    preferred_element_type=F32,
                ) + jnp.dot(
                    left_tiles[i, 1],
                    gathered[left_slot[2 * i + 1], pl.ds(second_start, WIN), lanes],
                    preferred_element_type=F32,
                )
                out_ref[pl.ds(row, tile), term * width + n : term * width + lanes.stop] = value.astype(BF16)
        return carry

    lax.fori_loop(0, steps, sector_step, 0)


def right_kernel(heights, halves, first_ref, rows_ref, cols_ref, left_ref, right_ref, *refs):
    out_ref = refs[-1]
    added = refs[:-1]
    full = out_ref.shape[0] // halves
    columns = cols_ref[pl.program_id(0)] - pl.program_id(1) * WIN

    @pl.when(columns <= 0)
    def _():
        out_ref[...] = jnp.zeros_like(out_ref)

    for half in range(halves):
        lower = 0
        for height in heights:
            count = rows_ref[half]

            @pl.when((columns > 0) & (count > lower) & (count <= height))
            def _(half=half, height=height):
                rows = slice(half * full, half * full + height)
                value = jnp.dot(left_ref[rows], right_ref[...], preferred_element_type=F32)
                for other in added:
                    value = value + other[rows].astype(F32)
                out_ref[rows] = value.astype(BF16)
                if height < full:
                    out_ref[half * full + height : (half + 1) * full] = jnp.zeros(
                        (full - height, out_ref.shape[1]), BF16
                    )

            lower = height


def unpack_kernel(group, row_start, row_size, col_start, col_shift, col_size, packed_ref, out_ref, select, rows):
    sectors, _, tile = select.shape

    @pl.when((pl.program_id(0) == 0) & (pl.program_id(1) == 0))
    def _():
        state = lax.broadcasted_iota(I32, (WIN, tile), 1)
        spot = lax.broadcasted_iota(I32, (WIN, tile), 0) - state
        for q in range(sectors):
            select[q] = jnp.where((spot == col_shift[q]) & (state < col_size[q]), 1.0, 0.0).astype(BF16)

    for u in range(group):
        sector = pl.program_id(1) * group + u
        start = pl.multiple_of(row_start[sector], 16)
        value = packed_ref[0, pl.ds(start, tile), :].astype(F32)
        keep = lax.broadcasted_iota(I32, value.shape, 0) < row_size[sector]
        rows[u * tile : (u + 1) * tile] = jnp.where(keep, value, 0.0).astype(BF16)
    for q in range(sectors):
        start = pl.multiple_of(col_start[q], 128)
        value = jnp.dot(rows[:, pl.ds(start, WIN)], select[q], preferred_element_type=F32)
        out_ref[0, :, q * tile : (q + 1) * tile] = value.astype(BF16)


def fast(caps, wavefunction, left_tiles, left_source, left_weight, left_sizes, right_tiles, right_source, right_weight, right_sizes):
    cap_row, cap_pair, cap_half, cap_col = caps
    vectors, rows_local, cols_local = wavefunction.shape
    terms, right_local, right_b, tile, _ = right_tiles.shape
    left_b = left_tiles.shape[2]
    left_devices = lax.axis_size("lsec")
    right_devices = lax.axis_size("rsec")
    left_local = rows_local // tile
    chain = left_devices // 2
    height = right_devices // 2
    left_place = lax.axis_index("lsec")
    right_place = lax.axis_index("rsec")
    side = left_place % 2
    place = left_place // 2
    core = right_place % 2
    tall = right_place // 2
    swap_side = [(i, i ^ 1) for i in range(left_devices)]
    swap_core = [(i, i ^ 1) for i in range(right_devices)]
    first_width = (cap_col // 128 + 1) // 2 * 128
    widths = [first_width, cap_col - first_width]
    bounds = [0, first_width, cap_col]

    own_sizes = lax.dynamic_slice_in_dim(left_sizes, left_place * left_local, left_local)
    pair_sizes = left_sizes.reshape(chain, 2 * left_local)
    pair_offset = exclusive(pair_sizes).reshape(-1)
    own_count = jnp.sum(own_sizes)
    rounded = (left_sizes + 15) // 16 * 16
    half_offset = exclusive(rounded.reshape(left_devices, left_local))
    half_count = jnp.sum(rounded.reshape(left_devices, left_local), axis=-1)
    column_offset = exclusive(right_sizes.reshape(right_devices, right_local)).reshape(-1)
    column_count = jnp.sum(right_sizes.reshape(right_devices, right_local), axis=-1)
    offsets = jnp.arange(tile, dtype=I32)

    def spread(starts, sizes):
        return jnp.where(offsets[None, :] < sizes[:, None], starts[:, None] + offsets[None, :], -1).reshape(-1)

    own_right = right_place * right_local
    col_sizes = lax.dynamic_slice_in_dim(right_sizes, own_right, right_local)
    col_starts = lax.dynamic_slice_in_dim(column_offset, own_right, right_local)
    col_index = spread(col_starts, col_sizes)
    col_select = one_hot(col_index, cap_col)
    pair_starts = lax.dynamic_slice_in_dim(pair_offset, left_place * left_local, left_local)
    local_index = spread(exclusive(own_sizes), own_sizes)
    pair_index = spread(pair_starts, own_sizes)

    def compact_right(tie):
        starts, tiles = after((col_starts, right_tiles), tie)
        return pl.pallas_call(
            compact_kernel,
            out_shape=jax.ShapeDtypeStruct((terms * right_b, cap_col, tile), BF16),
            grid_spec=pltpu.PrefetchScalarGridSpec(
                num_scalar_prefetch=1,
                grid=(terms, right_b),
                in_specs=[pl.BlockSpec((1, right_local, 1, tile, tile), lambda k, b, *_: (k, 0, b, 0, 0))],
                out_specs=pl.BlockSpec((1, cap_col, tile), lambda k, b, *_: (k * right_b + b, 0, 0)),
                scratch_shapes=[pltpu.VMEM((cap_col + tile, tile), F32)],
            ),
            cost_estimate=cost(1e6, 1e5),
        )(starts, tiles)

    with jax.named_scope("pack"):
        other = lax.dynamic_index_in_dim(wavefunction, 1 - side, 0, keepdims=False)
        other_rows = matmul(one_hot(local_index, cap_row).T, other).astype(BF16)
        incoming = []
        for n in range(2):
            outgoing = matmul(other_rows, col_select[:, bounds[n] : bounds[n + 1]]).astype(BF16)
            incoming.append(lax.ppermute(outgoing, "lsec", swap_side))
        compact = compact_right(outgoing)
        mine = lax.dynamic_index_in_dim(after(wavefunction, compact), side, 0, keepdims=False)
        mine_rows = matmul(one_hot(pair_index, cap_pair).T, mine).astype(BF16)
        pair_total = jnp.sum(lax.dynamic_index_in_dim(pair_sizes, place, 0, keepdims=False))
        partner_base = jnp.where(side == 0, own_count, 0)
        partner_count = pair_total - own_count
        spots = jnp.arange(cap_row, dtype=I32)
        partner_select = one_hot(jnp.where(spots < partner_count, partner_base + spots, -1), cap_pair).T
        pair = []
        for n in range(2):
            own_part = matmul(mine_rows, col_select[:, bounds[n] : bounds[n + 1]])
            pair.append((own_part + matmul(partner_select, incoming[n])).astype(BF16))

    upward = [[part] for part in pair]
    downward = [[part] for part in pair]
    hops = []

    def hop(n, *ties):
        up, down = after((upward[n][-1], downward[n][-1]), *ties)
        with jax.named_scope("chain"):
            upward[n].append(lax.ppermute(up, "lsec", [(i, i + 2) for i in range(left_devices - 2)]))
            downward[n].append(lax.ppermute(down, "lsec", [(i + 2, i) for i in range(left_devices - 2)]))
        hops.append((upward[n][-1], downward[n][-1]))

    def tall_permute(value, d):
        with jax.named_scope("right_exchange"):
            return lax.ppermute(
                value, "rsec", [(i, ((i // 2 - d) % height) * 2 + i % 2) for i in range(right_devices)]
            )

    def core_permute(value):
        with jax.named_scope("right_exchange"):
            return lax.ppermute(value, "rsec", swap_core)

    def prepare_left(tie):
        with jax.named_scope("left_exchange"):
            own_weight = lax.dynamic_slice_in_dim(left_weight, left_place * left_local, left_local, 1)
            left_scaled = (after(left_tiles, incoming[1]).astype(F32) * own_weight[..., None, None]).astype(BF16)
            left_other = lax.ppermute(left_scaled, "lsec", swap_side)
            left_scaled, left_other = after((left_scaled, left_other), tie)
            left_pair = jnp.where(
                side == 0, jnp.concatenate([left_scaled, left_other], 1), jnp.concatenate([left_other, left_scaled], 1)
            )
            source = lax.dynamic_slice_in_dim(left_source, place * 2 * left_local, 2 * left_local, 1)
            source = jnp.transpose(source, (1, 0, 2))
            source_offset = lookup(pair_offset, source)
            left_slot = source // (2 * left_local)
            left_start = jnp.minimum(source_offset // 16 * 16, cap_pair - WIN)
            source_size = lookup(left_sizes, source)
            moved = jnp.where(
                offsets < source_size[..., None], (source_offset - left_start)[..., None] + offsets, -1
            )
            left_shifted = jnp.einsum(
                "klbij,lkbjc->lkbic", left_pair, one_hot(moved, WIN), preferred_element_type=F32
            ).astype(BF16).reshape(2 * left_local * terms, left_b, tile, WIN)
        return left_slot, left_start, left_shifted

    def make_lists(tie):
        with jax.named_scope("lists"):
            both = after(listed, tie)
            both = jnp.transpose(jnp.stack(both), (1, 0, 3, 2, 4))
            slots = jnp.arange(right_devices, dtype=I32)
            groups = 2 * ((tall + slots // 2) % height) + (core + slots) % 2
            ordered = both[0].reshape(-1).astype(I32)
            weights = both[1].reshape(-1)
            items = ordered.shape[0]
            number = jnp.arange(items, dtype=I32)
            key = jnp.where(ordered // right_local == right_place, number, items + number)
            key, ordered, weights = lax.sort((key, ordered, weights), num_keys=1)
            active = key < items
            number = key % items
            item_slot = number // (right_local * per_sector)
            sector = (2 * ((tall + item_slot // 2) % height) + (core + item_slot) % 2) * right_local
            sector = sector + number // per_sector % right_local
            low = lookup(column_offset, sector)
            high = low + lookup(right_sizes, sector)
            from_offset = lookup(column_offset, ordered)
            window = jnp.minimum(from_offset // 128 * 128, cap_col - WIN)
            edges = jnp.arange(panels, dtype=I32) * WIN
            earlier = item_slot[None, None, :] < slots[:, None, None]
            same = item_slot[None, None, :] == slots[:, None, None]
            before = active & (earlier | (same & (high <= edges[None, :, None])))
            within = active & (earlier | (same & (low < edges[None, :, None] + WIN)))
            panel_first = jnp.sum(before.astype(I32), -1)
            panel_last = jnp.sum(within.astype(I32), -1)
            fields = (number % per_sector, low, high, window, from_offset - window, lookup(right_sizes, ordered), weights)
        return fields, panel_first, panel_last

    per_sector = terms * right_b
    panels = (cap_col + WIN - 1) // WIN
    rows = 2 * cap_half
    halves = lax.dynamic_slice_in_dim(half_offset, place * 2, 2, 0) + jnp.arange(2, dtype=I32)[:, None] * cap_half
    anywhere = pl.BlockSpec(memory_space=pl.ANY)

    def build(parts, d, lists, tie):
        fields, panel_first, panel_last = lists
        chosen = slice(2 * d, 2 * d + 2)
        scalars = (*fields, panel_first[chosen].reshape(-1), panel_last[chosen].reshape(-1))
        split = len(parts[0])
        inputs = after(parts[0] + parts[1], tie)
        specs = []
        for slot in range(2):
            for part in parts[slot]:
                specs.append(
                    pl.BlockSpec(
                        (part.shape[0], WIN, tile),
                        lambda s, p, *_, slot=slot: (0, jnp.where(s == slot, p, (panels - 1) * (1 - slot)), 0),
                    )
                )
        with jax.named_scope("build"):
            return pl.pallas_call(
                functools.partial(build_kernel, (widths, right_b, panels, split, fields[0].shape[0])),
                out_shape=[jax.ShapeDtypeStruct((terms * width, 2 * panels * WIN), BF16) for width in widths],
                grid_spec=pltpu.PrefetchScalarGridSpec(
                    num_scalar_prefetch=len(scalars),
                    grid=(2, panels),
                    in_specs=specs,
                    out_specs=[
                        pl.BlockSpec((terms * width, WIN), lambda s, p, *_: (0, s * panels + p)) for width in widths
                    ],
                    scratch_shapes=[pltpu.VMEM((per_sector, WIN, tile), BF16)],
                ),
                compiler_params=pltpu.CompilerParams(vmem_limit_bytes=VMEM_LIMIT),
                cost_estimate=cost(1e6, 1e5),
            )(*scalars, *inputs)

    def apply_left(n, left_parts):
        left_slot, left_start, left_shifted = left_parts
        blocks = upward[n] + downward[n][1:]
        scalars = (place.reshape(1), left_slot.reshape(-1), left_start.reshape(-1), halves.reshape(-1))
        width = widths[n]
        with jax.named_scope("apply_left"):
            return pl.pallas_call(
                functools.partial(left_kernel, (chain, terms, 2 * left_local, width)),
                out_shape=jax.ShapeDtypeStruct((rows + tile, terms * width), BF16),
                grid_spec=pltpu.PrefetchScalarGridSpec(
                    num_scalar_prefetch=len(scalars),
                    grid=(1,),
                    in_specs=[anywhere] * (len(blocks) + 1),
                    out_specs=pl.BlockSpec((rows + tile, terms * width), lambda i, *_: (0, 0)),
                    scratch_shapes=[
                        pltpu.VMEM((chain, cap_pair, width), BF16),
                        pltpu.VMEM((2 * left_local * terms, left_b, tile, WIN), BF16),
                        pltpu.SemaphoreType.DMA((2 * chain,)),
                    ],
                ),
                compiler_params=pltpu.CompilerParams(vmem_limit_bytes=VMEM_LIMIT),
                cost_estimate=cost(1e6, 1e5),
            )(*scalars, *blocks, left_shifted)

    own_list = jnp.stack([right_source.astype(F32), right_weight])
    listed = []
    for d in range(height):
        listed.append(tall_permute(own_list, d) if d else own_list)
        listed.append(core_permute(listed[-1]))
    near = core_permute(compact)
    far = [[[], []] for _ in range(1, height)]
    sent = []

    def send_far(*ties):
        term = len(sent)
        piece = after(compact[term * right_b : (term + 1) * right_b], *ties, *sent[-1:])
        for d in range(1, height):
            far[d - 1][0].append(tall_permute(piece, d))
        sent.append([far[d - 1][0][-1] for d in range(1, height)])

    send_far()
    hop(0)
    send_far(pair[0])
    hop(1, sent[0])
    send_far(pair[1])
    lists = make_lists(pair[1])
    built = [build([[compact], [near]], 0, lists, pair[1])]
    hop(0, lists, sent[1])
    for term in range(3, terms):
        send_far(lists)
    for d in range(1, height):
        far[d - 1][1] = [core_permute(piece) for piece in far[d - 1][0]]
    hop(1, built, sent[2])
    for d in range(1, height):
        built.append(build(far[d - 1], d, lists, hops[1]))
    for step in range(3, chain):
        hop(0, sent[3:] if step == 3 else [])
        if step == 3:
            left_parts = prepare_left(hops[2])
        hop(1, (left_parts, built) if step == 3 else [])
    product = apply_left(0, left_parts)
    span = panels * WIN
    heights = [h for h in range(640, cap_half, 128)] + [cap_half]
    half_rows = lax.dynamic_slice_in_dim(half_count, place * 2, 2, 0)

    def apply_right(left, right, slots, halves, first, row_counts, columns, added):
        width = left.shape[1]
        full = halves * cap_half
        number = columns.shape[0]
        block = pl.BlockSpec((full, WIN), lambda s, p, *_: (0, s * panels + p))
        scalars = (first.reshape(1), row_counts, columns)
        return pl.pallas_call(
            functools.partial(right_kernel, heights, halves),
            out_shape=jax.ShapeDtypeStruct((full, number * span), BF16),
            grid_spec=pltpu.PrefetchScalarGridSpec(
                num_scalar_prefetch=3,
                grid=(number, panels),
                in_specs=[
                    pl.BlockSpec((full, width), lambda s, p, first, *_: (first[0], 0)),
                    pl.BlockSpec((width, WIN), lambda s, p, *_: (0, (s + slots) * panels + p)),
                ]
                + (
                    [pl.BlockSpec((full, WIN), lambda s, p, first, *_: (first[0], (s + slots) * panels + p))]
                    if added
                    else []
                )
                + (
                    [pl.BlockSpec((full, WIN), lambda s, p, first, *_: (first[0], s * panels + p))]
                    if len(added) > 1
                    else []
                ),
                out_specs=block,
            ),
            compiler_params=pltpu.CompilerParams(vmem_limit_bytes=VMEM_LIMIT),
            cost_estimate=cost(1e6, 1e5),
        )(*scalars, left, right, *added)

    groups_of = [2 * ((tall + d) % height) for d in range(height)]
    slot_cols = [
        lookup(column_count, jnp.stack([groups_of[d] + core, groups_of[d] + 1 - core])) for d in range(height)
    ]
    zero = jnp.zeros((), I32)
    with jax.named_scope("apply_right"):
        partial = [
            apply_right(product, built[d][0], 0, 2, zero, half_rows, slot_cols[d], []) for d in range(height)
        ]
    product = apply_left(1, after(left_parts, partial))
    order = [1 - side, side]

    with jax.named_scope("apply_right"):
        crossed = {}
        last = product

        def cross(d, tie):
            away = apply_right(
                after(product, tie), built[d][1], 1, 2, zero, half_rows, slot_cols[d][1:], [partial[d]]
            )
            with jax.named_scope("reduce"):
                crossed[d] = lax.ppermute(away, "rsec", swap_core)
            return away

        def stays(h, d, tie):
            return apply_right(
                after(product, tie),
                built[d][1],
                0,
                1,
                order[h],
                lax.dynamic_slice_in_dim(half_rows, order[h], 1),
                slot_cols[d][:1],
                [partial[d], crossed[d]],
            )

        arrived = [[], []]
        for d in range(1, height):
            last = cross(d, last)
            for h in range(2):
                last = stays(h, d, last)
                with jax.named_scope("reduce"):
                    arrived[h].append(
                        lax.ppermute(
                            last, "rsec", [(i, ((i // 2 + d) % height) * 2 + i % 2) for i in range(right_devices)]
                        )
                    )
        last = cross(0, last)
        results = []
        for h in range(2):
            last = stays(h, 0, last)
            total = last.astype(F32)
            for value in arrived[h]:
                total = total + value.astype(F32)
            results.append(total.astype(BF16))
    given, kept = results
    with jax.named_scope("reduce"):
        taken = lax.ppermute(given, "lsec", swap_side)

    with jax.named_scope("unpack"):
        both = jnp.stack([jnp.where(side == 0, kept, taken), jnp.where(side == 0, taken, kept)])
        both = jnp.pad(both, ((0, 0), (0, tile), (0, 0)))
        col_window = jnp.minimum(col_starts // 128 * 128, cap_col - WIN)
        group = 4 if left_local % 4 == 0 else 1
        scalars = (
            lax.dynamic_index_in_dim(half_offset, left_place, 0, keepdims=False),
            own_sizes,
            col_window,
            col_starts - col_window,
            col_sizes,
        )
        return pl.pallas_call(
            functools.partial(unpack_kernel, group),
            out_shape=jax.ShapeDtypeStruct((vectors, rows_local, cols_local), BF16),
            grid_spec=pltpu.PrefetchScalarGridSpec(
                num_scalar_prefetch=len(scalars),
                grid=(vectors, left_local // group),
                in_specs=[pl.BlockSpec((1, cap_half + tile, span), lambda v, r, *_: (v, 0, 0))],
                out_specs=pl.BlockSpec((1, group * tile, cols_local), lambda v, r, *_: (v, r, 0)),
                scratch_shapes=[
                    pltpu.VMEM((right_local, WIN, tile), BF16),
                    pltpu.VMEM((group * tile, span), BF16),
                ],
            ),
            compiler_params=pltpu.CompilerParams(vmem_limit_bytes=VMEM_LIMIT),
        )(*scalars, both)


def local(wavefunction, left_tiles, left_source, left_weight, left_sizes, right_tiles, right_source, right_weight, right_sizes):
    _, rows_local, cols_local = wavefunction.shape
    left_devices = lax.axis_size("lsec")
    right_devices = lax.axis_size("rsec")

    def most(sizes, parts):
        here = jnp.arange(sizes.shape[0], dtype=I32) // (sizes.shape[0] // parts)
        return jnp.max(jnp.sum(jnp.where(here == jnp.arange(parts, dtype=I32)[:, None], sizes, 0), -1))

    most_rows = most(left_sizes, left_devices)
    most_half = most((left_sizes + 15) // 16 * 16, left_devices)
    most_pair = most(left_sizes, left_devices // 2)
    most_cols = most(right_sizes, right_devices)
    arguments = (wavefunction, left_tiles, left_source, left_weight, left_sizes, right_tiles, right_source, right_weight, right_sizes)
    branches = []
    choice = jnp.full((), len(LEVELS), I32)
    for level, (row, pair, half, col) in reversed(list(enumerate(LEVELS))):
        caps = (
            rows_local * row // 16,
            rows_local * pair // 16,
            rows_local * half // 16,
            cols_local * col // 16 // 128 * 128,
        )
        fits = (most_rows <= caps[0]) & (most_pair <= caps[1]) & (most_half <= caps[2]) & (most_cols <= caps[3])
        branches.insert(0, functools.partial(fast, caps))
        choice = jnp.where(fits, level, choice)
    return lax.switch(choice, [*branches, general], *arguments)


LEVELS = ((12, 20, 12, 10), (14, 22, 14, 11), (16, 24, 16, 12))


def solution(mesh):
    return jax.shard_map(
        local,
        mesh=mesh,
        in_specs=(
            P(None, "lsec", "rsec"),
            P(None, "lsec", None, None, None),
            P(),
            P(),
            P(),
            P(None, "rsec", None, None, None),
            P(None, "rsec", None),
            P(None, "rsec", None),
            P(),
        ),
        out_specs=P(None, "lsec", "rsec"),
        check_vma=False,
    )
```

```python
import functools

import jax
import jax.numpy as jnp
from jax import lax
from jax.experimental import pallas as pl
from jax.experimental.pallas import tpu as pltpu
from jax.sharding import PartitionSpec as P

F32 = jnp.float32
BF16 = jnp.bfloat16
I32 = jnp.int32
WIN = 256
VMEM_LIMIT = 60 * 1024 * 1024


def sector_mask(sizes, tile):
    offsets = jnp.arange(tile, dtype=jnp.int32)
    return (offsets[None, :] < sizes[:, None]).reshape(-1)


def scaled_tiles(tiles, weight):
    return (tiles.astype(jnp.float32) * weight[..., None, None]).astype(jnp.bfloat16)


def weighted_right(selected_rows, scaled):
    return jnp.einsum("vlqbs,qbts->vlqt", selected_rows, scaled, preferred_element_type=jnp.float32)


def left_rows(arranged, product_fragments, source, weight):
    total = None
    for term in range(product_fragments.shape[0]):
        selected_rows = jnp.take(arranged[:, :, :, term, :], source[term], axis=1)
        scaled = scaled_tiles(product_fragments[term], weight[term])
        part = jnp.einsum(
            "mbij,vmbjc->vmic", scaled, selected_rows, preferred_element_type=jnp.float32
        )
        total = part if total is None else total + part
    return total.reshape(total.shape[0], -1, total.shape[-1])


def general(
    wavefunction,
    left_tiles,
    left_source_sector,
    left_weight,
    left_sizes,
    right_tiles,
    right_source,
    right_weight,
    right_sizes,
):
    vectors, rows_local, cols_local = wavefunction.shape
    terms_count = right_tiles.shape[0]
    tile = right_tiles.shape[3]
    left_count = left_sizes.shape[0]
    right_count = right_sizes.shape[0]
    left_local = rows_local // tile
    right_local = cols_local // tile
    left_devices = lax.axis_size("lsec")
    width = cols_local // left_devices
    left_place = lax.axis_index("lsec")
    right_place = lax.axis_index("rsec")
    row_keep_mask = sector_mask(
        lax.dynamic_slice_in_dim(left_sizes, left_place * left_local, left_local), tile
    )
    col_keep = sector_mask(
        lax.dynamic_slice_in_dim(right_sizes, right_place * right_local, right_local), tile
    )
    masked = jnp.where(
        row_keep_mask[None, :, None] & col_keep[None, None, :],
        wavefunction,
        jnp.zeros((), wavefunction.dtype),
    )
    right_scaled = scaled_tiles(right_tiles, right_weight)
    gathered = lax.all_gather(masked, "rsec", axis=2, tiled=True)
    sector_block_list = gathered.reshape(vectors, rows_local, right_count, tile)
    products = []
    for term in range(terms_count):
        selected_rows = jnp.take(sector_block_list, right_source[term], axis=2)
        products.append(weighted_right(selected_rows, right_scaled[term]))
    rounded = [
        item.astype(jnp.bfloat16).reshape(vectors, rows_local, left_devices, width)
        for item in products
    ]
    outgoing = jnp.stack(rounded, axis=3)
    exchanged_values = lax.all_to_all(
        outgoing.reshape(vectors, rows_local, -1), "lsec", split_axis=2, concat_axis=1, tiled=True
    )
    arranged = exchanged_values.reshape(vectors, left_count, tile, terms_count, width)
    sigma_part = left_rows(
        arranged,
        lax.all_gather(left_tiles, "lsec", axis=1, tiled=True),
        left_source_sector,
        left_weight,
    )
    row_all = sector_mask(left_sizes, tile)
    columns = right_place * cols_local + left_place * width + jnp.arange(width, dtype=jnp.int32)
    column_sizes = jnp.take(right_sizes, columns // tile)
    column_keep = columns % tile < column_sizes
    result = jnp.where(
        row_all[None, :, None] & column_keep[None, None, :],
        sigma_part,
        jnp.zeros((), sigma_part.dtype),
    )
    return lax.all_to_all(
        result.astype(jnp.bfloat16), "lsec", split_axis=1, concat_axis=2, tiled=True
    )


def exclusive(values):
    return jnp.cumsum(values, axis=-1) - values


def one_hot(index, count):
    return (index[..., None] == jnp.arange(count, dtype=I32)).astype(BF16)


def lookup(table, index):
    return jnp.sum(jnp.where(index[..., None] == jnp.arange(table.shape[0], dtype=I32), table, 0), axis=-1)


def matmul(a, b):
    return jnp.matmul(a, b, preferred_element_type=F32)


def after(value, *others):
    return lax.optimization_barrier((value, others))[0]


def cost(flops, bytes_accessed):
    return pl.CostEstimate(flops=int(flops), bytes_accessed=int(bytes_accessed), transcendentals=0)


def compact_kernel(start_ref, tiles_ref, out_ref, rows_ref):
    tile = tiles_ref.shape[3]

    @pl.when((pl.program_id(0) == 0) & (pl.program_id(1) == 0))
    def _():
        rows_ref[...] = jnp.zeros_like(rows_ref)

    for q in range(tiles_ref.shape[1]):
        rows_ref[pl.ds(start_ref[q], tile), :] = tiles_ref[0, q, 0].astype(F32)
    out_ref[0] = rows_ref[: out_ref.shape[1], :].astype(BF16)


def build_kernel(dims, item_kb, item_lo, item_hi, item_win, item_shift, item_size, item_weight, panel_first, panel_last, *refs):
    widths, right_b, panels, split, items = dims
    outs = refs[-1 - len(widths) : -1]
    held = refs[-1]
    parts = refs[: -1 - len(widths)]
    tile = held.shape[2]
    here = pl.program_id(0) * panels + pl.program_id(1)
    for slot in range(2):
        @pl.when(pl.program_id(0) == slot)
        def _(slot=slot):
            base = 0
            for part in parts[slot * split : (slot + 1) * split]:
                held[base : base + part.shape[0]] = part[...]
                base += part.shape[0]

    for out in outs:
        out[...] = jnp.zeros_like(out)
    column = lax.broadcasted_iota(I32, (WIN, tile), 0) + pl.program_id(1) * WIN
    source = lax.broadcasted_iota(I32, (WIN, tile), 1)
    target = lax.broadcasted_iota(I32, (WIN, tile), 0) - source
    first = panel_first[here]
    last = panel_last[here]

    def step(g, carry):
        values = []
        for u in range(2):
            raw = first + 2 * g + u
            it = jnp.minimum(raw, items - 1)
            kb = item_kb[it]
            block = (held[kb].astype(F32) * item_weight[it])
            block = jnp.where((column >= item_lo[it]) & (column < item_hi[it]), block, 0.0).astype(BF16)
            size = jnp.where(raw < last, item_size[it], 0)
            shift = jnp.where((target == item_shift[it]) & (source < size), 1.0, 0.0).astype(BF16)
            value = lax.dot_general(shift, block, (((1,), (1,)), ((), ())), preferred_element_type=F32)
            values.append((kb // right_b, item_win[it], value.astype(BF16)))
        for term, window, value in values:
            for part in range(WIN // tile):
                start = window + part * tile
                base = 0
                for out, width in zip(outs, widths):
                    @pl.when((start >= base) & (start < base + width))
                    def _(out=out, width=width, base=base, part=part, term=term, start=start, value=value):
                        row = jnp.clip(term * width + start - base, 0, out.shape[0] - tile)
                        row = pl.multiple_of(row, tile)
                        out[pl.ds(row, tile), :] += value[part * tile : (part + 1) * tile]
                    base += width
        return carry

    lax.fori_loop(0, (last - first + 1) // 2, step, 0)


def left_kernel(dims, place_ref, left_slot, left_start, row_start, *refs):
    chain, terms, steps, width = dims
    blocks = refs[: 2 * chain - 1]
    left_ref, out_ref, gathered, left_tiles, sem = refs[2 * chain - 1 :]
    tile = left_ref.shape[2]
    place = place_ref[0]

    def each(action):
        action(pltpu.make_async_copy(blocks[0], gathered.at[place], sem.at[0]))
        for d in range(1, chain):
            @pl.when(place - d >= 0)
            def _():
                action(pltpu.make_async_copy(blocks[d], gathered.at[jnp.maximum(place - d, 0)], sem.at[d]))

            @pl.when(place + d < chain)
            def _():
                action(
                    pltpu.make_async_copy(
                        blocks[chain - 1 + d], gathered.at[jnp.minimum(place + d, chain - 1)], sem.at[chain - 1 + d]
                    )
                )
        action(pltpu.make_async_copy(left_ref, left_tiles, sem.at[2 * chain - 1]))

    each(lambda copy: copy.start())
    out_ref[...] = jnp.zeros_like(out_ref)
    each(lambda copy: copy.wait())

    def sector_step(sector, carry):
        row = pl.multiple_of(row_start[sector], 16)
        for term in range(terms):
            i = sector * terms + term
            first_start = pl.multiple_of(left_start[2 * i], 16)
            second_start = pl.multiple_of(left_start[2 * i + 1], 16)
            for n in range(0, width, WIN):
                lanes = slice(n, min(n + WIN, width))
                value = jnp.dot(
                    left_tiles[i, 0],
                    gathered[left_slot[2 * i], pl.ds(first_start, WIN), lanes],
                    preferred_element_type=F32,
                ) + jnp.dot(
                    left_tiles[i, 1],
                    gathered[left_slot[2 * i + 1], pl.ds(second_start, WIN), lanes],
                    preferred_element_type=F32,
                )
                out_ref[pl.ds(row, tile), term * width + n : term * width + lanes.stop] = value.astype(BF16)
        return carry

    lax.fori_loop(0, steps, sector_step, 0)


def right_kernel(heights, halves, first_ref, rows_ref, cols_ref, left_ref, right_ref, *refs):
    out_ref = refs[-1]
    added = refs[:-1]
    full = out_ref.shape[0] // halves
    columns = cols_ref[pl.program_id(0)] - pl.program_id(1) * WIN

    @pl.when(columns <= 0)
    def _():
        out_ref[...] = jnp.zeros_like(out_ref)

    for half in range(halves):
        lower = 0
        for height in heights:
            count = rows_ref[half]

            @pl.when((columns > 0) & (count > lower) & (count <= height))
            def _(half=half, height=height):
                rows = slice(half * full, half * full + height)
                value = jnp.dot(left_ref[rows], right_ref[...], preferred_element_type=F32)
                for other in added:
                    value = value + other[rows].astype(F32)
                out_ref[rows] = value.astype(BF16)
                if height < full:
                    out_ref[half * full + height : (half + 1) * full] = jnp.zeros(
                        (full - height, out_ref.shape[1]), BF16
                    )

            lower = height


def unpack_kernel(group, row_start, row_size, col_start, col_shift, col_size, packed_ref, out_ref, select, rows):
    sectors, _, tile = select.shape

    @pl.when((pl.program_id(0) == 0) & (pl.program_id(1) == 0))
    def _():
        state = lax.broadcasted_iota(I32, (WIN, tile), 1)
        spot = lax.broadcasted_iota(I32, (WIN, tile), 0) - state
        for q in range(sectors):
            select[q] = jnp.where((spot == col_shift[q]) & (state < col_size[q]), 1.0, 0.0).astype(BF16)

    for u in range(group):
        sector = pl.program_id(1) * group + u
        start = pl.multiple_of(row_start[sector], 16)
        value = packed_ref[0, pl.ds(start, tile), :].astype(F32)
        keep = lax.broadcasted_iota(I32, value.shape, 0) < row_size[sector]
        rows[u * tile : (u + 1) * tile] = jnp.where(keep, value, 0.0).astype(BF16)
    for q in range(sectors):
        start = pl.multiple_of(col_start[q], 128)
        value = jnp.dot(rows[:, pl.ds(start, WIN)], select[q], preferred_element_type=F32)
        out_ref[0, :, q * tile : (q + 1) * tile] = value.astype(BF16)


def fast(caps, wavefunction, left_tiles, left_source, left_weight, left_sizes, right_tiles, right_source, right_weight, right_sizes):
    cap_row, cap_pair, cap_half, cap_col = caps
    vectors, rows_local, cols_local = wavefunction.shape
    terms, right_local, right_b, tile, _ = right_tiles.shape
    left_b = left_tiles.shape[2]
    left_devices = lax.axis_size("lsec")
    right_devices = lax.axis_size("rsec")
    left_local = rows_local // tile
    chain = left_devices // 2
    height = right_devices // 2
    left_place = lax.axis_index("lsec")
    right_place = lax.axis_index("rsec")
    side = left_place % 2
    place = left_place // 2
    core = right_place % 2
    tall = right_place // 2
    swap_side = [(i, i ^ 1) for i in range(left_devices)]
    swap_core = [(i, i ^ 1) for i in range(right_devices)]
    first_width = (cap_col // 128 + 1) // 2 * 128
    widths = [first_width, cap_col - first_width]
    bounds = [0, first_width, cap_col]

    own_sizes = lax.dynamic_slice_in_dim(left_sizes, left_place * left_local, left_local)
    pair_sizes = left_sizes.reshape(chain, 2 * left_local)
    pair_offset = exclusive(pair_sizes).reshape(-1)
    own_count = jnp.sum(own_sizes)
    rounded = (left_sizes + 15) // 16 * 16
    half_offset = exclusive(rounded.reshape(left_devices, left_local))
    half_count = jnp.sum(rounded.reshape(left_devices, left_local), axis=-1)
    column_offset = exclusive(right_sizes.reshape(right_devices, right_local)).reshape(-1)
    column_count = jnp.sum(right_sizes.reshape(right_devices, right_local), axis=-1)
    offsets = jnp.arange(tile, dtype=I32)

    def spread(starts, sizes):
        return jnp.where(offsets[None, :] < sizes[:, None], starts[:, None] + offsets[None, :], -1).reshape(-1)

    own_right = right_place * right_local
    col_sizes = lax.dynamic_slice_in_dim(right_sizes, own_right, right_local)
    col_starts = lax.dynamic_slice_in_dim(column_offset, own_right, right_local)
    col_index = spread(col_starts, col_sizes)
    col_select = one_hot(col_index, cap_col)
    pair_starts = lax.dynamic_slice_in_dim(pair_offset, left_place * left_local, left_local)
    local_index = spread(exclusive(own_sizes), own_sizes)
    pair_index = spread(pair_starts, own_sizes)

    def compact_right(tie):
        starts, tiles = after((col_starts, right_tiles), tie)
        return pl.pallas_call(
            compact_kernel,
            out_shape=jax.ShapeDtypeStruct((terms * right_b, cap_col, tile), BF16),
            grid_spec=pltpu.PrefetchScalarGridSpec(
                num_scalar_prefetch=1,
                grid=(terms, right_b),
                in_specs=[pl.BlockSpec((1, right_local, 1, tile, tile), lambda k, b, *_: (k, 0, b, 0, 0))],
                out_specs=pl.BlockSpec((1, cap_col, tile), lambda k, b, *_: (k * right_b + b, 0, 0)),
                scratch_shapes=[pltpu.VMEM((cap_col + tile, tile), F32)],
            ),
            cost_estimate=cost(1e6, 1e5),
        )(starts, tiles)

    with jax.named_scope("pack"):
        other = lax.dynamic_index_in_dim(wavefunction, 1 - side, 0, keepdims=False)
        other_rows = matmul(one_hot(local_index, cap_row).T, other).astype(BF16)
        incoming = []
        for n in range(2):
            outgoing = matmul(other_rows, col_select[:, bounds[n] : bounds[n + 1]]).astype(BF16)
            incoming.append(lax.ppermute(outgoing, "lsec", swap_side))
        compact = compact_right(outgoing)
        mine = lax.dynamic_index_in_dim(after(wavefunction, compact), side, 0, keepdims=False)
        mine_rows = matmul(one_hot(pair_index, cap_pair).T, mine).astype(BF16)
        pair_total = jnp.sum(lax.dynamic_index_in_dim(pair_sizes, place, 0, keepdims=False))
        partner_base = jnp.where(side == 0, own_count, 0)
        partner_count = pair_total - own_count
        spots = jnp.arange(cap_row, dtype=I32)
        partner_select = one_hot(jnp.where(spots < partner_count, partner_base + spots, -1), cap_pair).T
        pair = []
        for n in range(2):
            own_part = matmul(mine_rows, col_select[:, bounds[n] : bounds[n + 1]])
            pair.append((own_part + matmul(partner_select, incoming[n])).astype(BF16))

    upward = [[part] for part in pair]
    downward = [[part] for part in pair]
    hops = []

    def hop(n, *ties):
        up, down = after((upward[n][-1], downward[n][-1]), *ties)
        with jax.named_scope("chain"):
            upward[n].append(lax.ppermute(up, "lsec", [(i, i + 2) for i in range(left_devices - 2)]))
            downward[n].append(lax.ppermute(down, "lsec", [(i + 2, i) for i in range(left_devices - 2)]))
        hops.append((upward[n][-1], downward[n][-1]))

    def tall_permute(value, d):
        with jax.named_scope("right_exchange"):
            return lax.ppermute(
                value, "rsec", [(i, ((i // 2 - d) % height) * 2 + i % 2) for i in range(right_devices)]
            )

    def core_permute(value):
        with jax.named_scope("right_exchange"):
            return lax.ppermute(value, "rsec", swap_core)

    def prepare_left(tie):
        with jax.named_scope("left_exchange"):
            own_weight = lax.dynamic_slice_in_dim(left_weight, left_place * left_local, left_local, 1)
            left_scaled = (after(left_tiles, incoming[1]).astype(F32) * own_weight[..., None, None]).astype(BF16)
            left_other = lax.ppermute(left_scaled, "lsec", swap_side)
            left_scaled, left_other = after((left_scaled, left_other), tie)
            left_pair = jnp.where(
                side == 0, jnp.concatenate([left_scaled, left_other], 1), jnp.concatenate([left_other, left_scaled], 1)
            )
            source = lax.dynamic_slice_in_dim(left_source, place * 2 * left_local, 2 * left_local, 1)
            source = jnp.transpose(source, (1, 0, 2))
            source_offset = lookup(pair_offset, source)
            left_slot = source // (2 * left_local)
            left_start = jnp.minimum(source_offset // 16 * 16, cap_pair - WIN)
            source_size = lookup(left_sizes, source)
            moved = jnp.where(
                offsets < source_size[..., None], (source_offset - left_start)[..., None] + offsets, -1
            )
            left_shifted = jnp.einsum(
                "klbij,lkbjc->lkbic", left_pair, one_hot(moved, WIN), preferred_element_type=F32
            ).astype(BF16).reshape(2 * left_local * terms, left_b, tile, WIN)
        return left_slot, left_start, left_shifted

    def make_lists(tie):
        with jax.named_scope("lists"):
            both = after(listed, tie)
            both = jnp.transpose(jnp.stack(both), (1, 0, 3, 2, 4))
            slots = jnp.arange(right_devices, dtype=I32)
            groups = 2 * ((tall + slots // 2) % height) + (core + slots) % 2
            ordered = both[0].reshape(-1).astype(I32)
            weights = both[1].reshape(-1)
            items = ordered.shape[0]
            number = jnp.arange(items, dtype=I32)
            key = jnp.where(ordered // right_local == right_place, number, items + number)
            key, ordered, weights = lax.sort((key, ordered, weights), num_keys=1)
            active = key < items
            number = key % items
            item_slot = number // (right_local * per_sector)
            sector = (2 * ((tall + item_slot // 2) % height) + (core + item_slot) % 2) * right_local
            sector = sector + number // per_sector % right_local
            low = lookup(column_offset, sector)
            high = low + lookup(right_sizes, sector)
            from_offset = lookup(column_offset, ordered)
            window = jnp.minimum(from_offset // 128 * 128, cap_col - WIN)
            edges = jnp.arange(panels, dtype=I32) * WIN
            earlier = item_slot[None, None, :] < slots[:, None, None]
            same = item_slot[None, None, :] == slots[:, None, None]
            before = active & (earlier | (same & (high <= edges[None, :, None])))
            within = active & (earlier | (same & (low < edges[None, :, None] + WIN)))
            panel_first = jnp.sum(before.astype(I32), -1)
            panel_last = jnp.sum(within.astype(I32), -1)
            fields = (number % per_sector, low, high, window, from_offset - window, lookup(right_sizes, ordered), weights)
        return fields, panel_first, panel_last

    per_sector = terms * right_b
    panels = (cap_col + WIN - 1) // WIN
    rows = 2 * cap_half
    halves = lax.dynamic_slice_in_dim(half_offset, place * 2, 2, 0) + jnp.arange(2, dtype=I32)[:, None] * cap_half
    anywhere = pl.BlockSpec(memory_space=pl.ANY)

    def build(parts, d, lists, tie):
        fields, panel_first, panel_last = lists
        chosen = slice(2 * d, 2 * d + 2)
        scalars = (*fields, panel_first[chosen].reshape(-1), panel_last[chosen].reshape(-1))
        split = len(parts[0])
        inputs = after(parts[0] + parts[1], tie)
        specs = []
        for slot in range(2):
            for part in parts[slot]:
                specs.append(
                    pl.BlockSpec(
                        (part.shape[0], WIN, tile),
                        lambda s, p, *_, slot=slot: (0, jnp.where(s == slot, p, (panels - 1) * (1 - slot)), 0),
                    )
                )
        with jax.named_scope("build"):
            return pl.pallas_call(
                functools.partial(build_kernel, (widths, right_b, panels, split, fields[0].shape[0])),
                out_shape=[jax.ShapeDtypeStruct((terms * width, 2 * panels * WIN), BF16) for width in widths],
                grid_spec=pltpu.PrefetchScalarGridSpec(
                    num_scalar_prefetch=len(scalars),
                    grid=(2, panels),
                    in_specs=specs,
                    out_specs=[
                        pl.BlockSpec((terms * width, WIN), lambda s, p, *_: (0, s * panels + p)) for width in widths
                    ],
                    scratch_shapes=[pltpu.VMEM((per_sector, WIN, tile), BF16)],
                ),
                compiler_params=pltpu.CompilerParams(vmem_limit_bytes=VMEM_LIMIT),
                cost_estimate=cost(1e6, 1e5),
            )(*scalars, *inputs)

    def apply_left(n, left_parts):
        left_slot, left_start, left_shifted = left_parts
        blocks = upward[n] + downward[n][1:]
        scalars = (place.reshape(1), left_slot.reshape(-1), left_start.reshape(-1), halves.reshape(-1))
        width = widths[n]
        with jax.named_scope("apply_left"):
            return pl.pallas_call(
                functools.partial(left_kernel, (chain, terms, 2 * left_local, width)),
                out_shape=jax.ShapeDtypeStruct((rows + tile, terms * width), BF16),
                grid_spec=pltpu.PrefetchScalarGridSpec(
                    num_scalar_prefetch=len(scalars),
                    grid=(1,),
                    in_specs=[anywhere] * (len(blocks) + 1),
                    out_specs=pl.BlockSpec((rows + tile, terms * width), lambda i, *_: (0, 0)),
                    scratch_shapes=[
                        pltpu.VMEM((chain, cap_pair, width), BF16),
                        pltpu.VMEM((2 * left_local * terms, left_b, tile, WIN), BF16),
                        pltpu.SemaphoreType.DMA((2 * chain,)),
                    ],
                ),
                compiler_params=pltpu.CompilerParams(vmem_limit_bytes=VMEM_LIMIT),
                cost_estimate=cost(1e6, 1e5),
            )(*scalars, *blocks, left_shifted)

    own_list = jnp.stack([right_source.astype(F32), right_weight])
    listed = []
    for d in range(height):
        listed.append(tall_permute(own_list, d) if d else own_list)
        listed.append(core_permute(listed[-1]))
    near = core_permute(compact)
    far = [[[], []] for _ in range(1, height)]
    sent = []

    def send_far(*ties):
        term = len(sent)
        piece = after(compact[term * right_b : (term + 1) * right_b], *ties, *sent[-1:])
        for d in range(1, height):
            far[d - 1][0].append(tall_permute(piece, d))
        sent.append([far[d - 1][0][-1] for d in range(1, height)])

    send_far()
    hop(0)
    send_far(pair[0])
    hop(1, sent[0])
    send_far(pair[1])
    lists = make_lists(pair[1])
    built = [build([[compact], [near]], 0, lists, pair[1])]
    hop(0, lists, sent[1])
    for term in range(3, terms):
        send_far(lists)
    for d in range(1, height):
        far[d - 1][1] = [core_permute(piece) for piece in far[d - 1][0]]
    hop(1, built, sent[2])
    for d in range(1, height):
        built.append(build(far[d - 1], d, lists, hops[1]))
    for step in range(3, chain):
        hop(0, sent[3:] if step == 3 else [])
        if step == 3:
            left_parts = prepare_left(hops[2])
        hop(1, (left_parts, built) if step == 3 else [])
    product = apply_left(0, left_parts)
    span = panels * WIN
    heights = [h for h in range(640, cap_half, 128)] + [cap_half]
    half_rows = lax.dynamic_slice_in_dim(half_count, place * 2, 2, 0)

    def apply_right(left, right, slots, halves, first, row_counts, columns, added):
        width = left.shape[1]
        full = halves * cap_half
        number = columns.shape[0]
        block = pl.BlockSpec((full, WIN), lambda s, p, *_: (0, s * panels + p))
        scalars = (first.reshape(1), row_counts, columns)
        return pl.pallas_call(
            functools.partial(right_kernel, heights, halves),
            out_shape=jax.ShapeDtypeStruct((full, number * span), BF16),
            grid_spec=pltpu.PrefetchScalarGridSpec(
                num_scalar_prefetch=3,
                grid=(number, panels),
                in_specs=[
                    pl.BlockSpec((full, width), lambda s, p, first, *_: (first[0], 0)),
                    pl.BlockSpec((width, WIN), lambda s, p, *_: (0, (s + slots) * panels + p)),
                ]
                + (
                    [pl.BlockSpec((full, WIN), lambda s, p, first, *_: (first[0], (s + slots) * panels + p))]
                    if added
                    else []
                )
                + (
                    [pl.BlockSpec((full, WIN), lambda s, p, first, *_: (first[0], s * panels + p))]
                    if len(added) > 1
                    else []
                ),
                out_specs=block,
            ),
            compiler_params=pltpu.CompilerParams(vmem_limit_bytes=VMEM_LIMIT),
            cost_estimate=cost(1e6, 1e5),
        )(*scalars, left, right, *added)

    groups_of = [2 * ((tall + d) % height) for d in range(height)]
    slot_cols = [
        lookup(column_count, jnp.stack([groups_of[d] + core, groups_of[d] + 1 - core])) for d in range(height)
    ]
    zero = jnp.zeros((), I32)
    with jax.named_scope("apply_right"):
        partial = [
            apply_right(product, built[d][0], 0, 2, zero, half_rows, slot_cols[d], []) for d in range(height)
        ]
    product = apply_left(1, after(left_parts, partial))
    order = [1 - side, side]

    with jax.named_scope("apply_right"):
        crossed = {}
        last = product

        def cross(d, tie):
            away = apply_right(
                after(product, tie), built[d][1], 1, 2, zero, half_rows, slot_cols[d][1:], [partial[d]]
            )
            with jax.named_scope("reduce"):
                crossed[d] = lax.ppermute(away, "rsec", swap_core)
            return away

        def stays(h, d, tie):
            return apply_right(
                after(product, tie),
                built[d][1],
                0,
                1,
                order[h],
                lax.dynamic_slice_in_dim(half_rows, order[h], 1),
                slot_cols[d][:1],
                [partial[d], crossed[d]],
            )

        for d in list(range(1, height)) + [0]:
            last = cross(d, last)
        arrived = [[], []]
        sums = []
        for h in range(2):
            for d in range(1, height):
                last = stays(h, d, last)
                with jax.named_scope("reduce"):
                    arrived[h].append(
                        lax.ppermute(
                            last, "rsec", [(i, ((i // 2 + d) % height) * 2 + i % 2) for i in range(right_devices)]
                        )
                    )
            if sums:
                sums[0] = after(sums[0], last)
            last = stays(h, 0, last)
            sums.append(last)
        results = []
        for h in range(2):
            total = sums[h].astype(F32)
            for value in arrived[h]:
                total = total + value.astype(F32)
            results.append(total.astype(BF16))
    given, kept = results
    with jax.named_scope("reduce"):
        taken = lax.ppermute(given, "lsec", swap_side)

    with jax.named_scope("unpack"):
        both = jnp.stack([jnp.where(side == 0, kept, taken), jnp.where(side == 0, taken, kept)])
        both = jnp.pad(both, ((0, 0), (0, tile), (0, 0)))
        col_window = jnp.minimum(col_starts // 128 * 128, cap_col - WIN)
        group = 4 if left_local % 4 == 0 else 1
        scalars = (
            lax.dynamic_index_in_dim(half_offset, left_place, 0, keepdims=False),
            own_sizes,
            col_window,
            col_starts - col_window,
            col_sizes,
        )
        return pl.pallas_call(
            functools.partial(unpack_kernel, group),
            out_shape=jax.ShapeDtypeStruct((vectors, rows_local, cols_local), BF16),
            grid_spec=pltpu.PrefetchScalarGridSpec(
                num_scalar_prefetch=len(scalars),
                grid=(vectors, left_local // group),
                in_specs=[pl.BlockSpec((1, cap_half + tile, span), lambda v, r, *_: (v, 0, 0))],
                out_specs=pl.BlockSpec((1, group * tile, cols_local), lambda v, r, *_: (v, r, 0)),
                scratch_shapes=[
                    pltpu.VMEM((right_local, WIN, tile), BF16),
                    pltpu.VMEM((group * tile, span), BF16),
                ],
            ),
            compiler_params=pltpu.CompilerParams(vmem_limit_bytes=VMEM_LIMIT),
        )(*scalars, both)


def local(wavefunction, left_tiles, left_source, left_weight, left_sizes, right_tiles, right_source, right_weight, right_sizes):
    _, rows_local, cols_local = wavefunction.shape
    left_devices = lax.axis_size("lsec")
    right_devices = lax.axis_size("rsec")

    def most(sizes, parts):
        here = jnp.arange(sizes.shape[0], dtype=I32) // (sizes.shape[0] // parts)
        return jnp.max(jnp.sum(jnp.where(here == jnp.arange(parts, dtype=I32)[:, None], sizes, 0), -1))

    most_rows = most(left_sizes, left_devices)
    most_half = most((left_sizes + 15) // 16 * 16, left_devices)
    most_pair = most(left_sizes, left_devices // 2)
    most_cols = most(right_sizes, right_devices)
    arguments = (wavefunction, left_tiles, left_source, left_weight, left_sizes, right_tiles, right_source, right_weight, right_sizes)
    branches = []
    choice = jnp.full((), len(LEVELS), I32)
    for level, (row, pair, half, col) in reversed(list(enumerate(LEVELS))):
        caps = (
            rows_local * row // 16,
            rows_local * pair // 16,
            rows_local * half // 16,
            cols_local * col // 16 // 128 * 128,
        )
        fits = (most_rows <= caps[0]) & (most_pair <= caps[1]) & (most_half <= caps[2]) & (most_cols <= caps[3])
        branches.insert(0, functools.partial(fast, caps))
        choice = jnp.where(fits, level, choice)
    return lax.switch(choice, [*branches, general], *arguments)


LEVELS = ((12, 20, 12, 10), (14, 22, 14, 10), (14, 22, 14, 11), (16, 24, 16, 12))


def solution(mesh):
    return jax.shard_map(
        local,
        mesh=mesh,
        in_specs=(
            P(None, "lsec", "rsec"),
            P(None, "lsec", None, None, None),
            P(),
            P(),
            P(),
            P(None, "rsec", None, None, None),
            P(None, "rsec", None),
            P(None, "rsec", None),
            P(),
        ),
        out_specs=P(None, "lsec", "rsec"),
        check_vma=False,
    )
```
